256 devices in a mesh: ctx: 32 (over x, z), head: 8 (over y, core).
Axes of the slice: x: 4, y: 4, z: 8, core: 2. Of those that a mesh axis runs over, the one named last changes fastest.
Arguments:
- q_clean: bfloat16 [8192, 4096], P(('ctx', 'head')), may hold values from -14 to 14, as said below
- k_clean: bfloat16 [8192, 1024], P(('ctx', 'head')), may hold values from -14 to 14, as said below
- v_clean: bfloat16 [8192, 1024], P(('ctx', 'head')), may hold values from -6 to 6
- q_noised: bfloat16 [8192, 4096], P(('ctx', 'head')), may hold values from -14 to 14, as said below
- masked: int32 [8192], P('ctx'), may hold values 0 or 1
- noise_level: int32 [256], P('ctx'), may hold values from 0 to 7
- mask_key: bfloat16 [8, 1024], P(None, 'head'), may hold values from -6 to 6
- mask_value: bfloat16 [8, 1024], P(None, 'head'), may hold values from -6 to 6
- d_clean: bfloat16 [8192, 4096], P(('ctx', 'head')), may hold values from -6 to 6
- d_noised: bfloat16 [8192, 4096], P(('ctx', 'head')), may hold values from -6 to 6
Outputs:
- out_clean: bfloat16 [8192, 4096], P(('ctx', 'head'))
- out_noised: bfloat16 [8192, 4096], P(('ctx', 'head'))
- dq_clean: bfloat16 [8192, 4096], P(('ctx', 'head'))
- dq_noised: bfloat16 [8192, 4096], P(('ctx', 'head'))
- dk_clean: bfloat16 [8192, 1024], P(('ctx', 'head'))
- dv_clean: bfloat16 [8192, 1024], P(('ctx', 'head'))
The draws below stay inside these ranges and needn't reach their ends.
Inputs may be any that keep to these rules, and one draw needn't show every extreme that they name: `q_clean`: bounded entries. `k_clean`: bounded entries. `q_noised`: bounded entries.
All inputs are finite; a program needn't handle non-finite values. No bound on the sum of `masked` on one device may be relied on, other than what follows from the above.
Results may differ from the reference program's by a relative error of at most 0.029.
Values may be sent and summed in bfloat16 or wider, within the bound.
No kernel may reach another device: no remote copies, remote signals or barrier semaphores. Data moves between devices by JAX's collectives and lax.ppermute only.
A program may use at most 128 MiB of HBM per device.

```python
import jax
import jax.numpy as jnp
from jax import lax

QH = 32
KVH = 8
HD = 128
BLOCK = 32
LEVELS = 8
SEQ = 8192


def draw_q_clean(key, part):
    key = jax.random.fold_in(key, 2)
    result = jnp.clip(jax.random.normal(key, (SEQ, QH * HD), jnp.float32), -6.0, 6.0)
    return result.astype(jnp.bfloat16)


def draw_q_noised(key, part):
    key = jax.random.fold_in(key, 3)
    result = jnp.clip(jax.random.normal(key, (SEQ, QH * HD), jnp.float32), -6.0, 6.0)
    return result.astype(jnp.bfloat16)


def draw_k_clean(key, part):
    key = jax.random.fold_in(key, 1)
    result = jnp.clip(jax.random.normal(key, (SEQ, KVH * HD), jnp.float32), -6.0, 6.0)
    return result.astype(jnp.bfloat16)


def with_ends(values, own_key, low, top_value):
    place = [jax.random.randint(jax.random.fold_in(own_key, axis), (), 0, length) for axis, length in enumerate(values.shape)]
    widest = values.shape.index(max(values.shape))
    beside = place[:widest] + [(place[widest] + 1) % values.shape[widest]] + place[widest + 1:]
    return values.at[tuple(place)].set(low).at[tuple(beside)].set(top_value)


def block_scale(rng, dims, split, low, top_value):
    loudness = 1.0
    for axis_at, blocks in split:
        heights = jax.random.uniform(jax.random.fold_in(jax.random.fold_in(rng, 6), axis_at), (blocks,), jnp.float32, low / len(split), top_value / len(split))
        loudness = loudness * jnp.repeat(jnp.exp(heights), dims[axis_at] // blocks).reshape((-1,) + (1,) * (len(dims) - 1 - axis_at))
    return loudness


def centred(key, extent, deviation, bound, shards=(), kind=jnp.bfloat16):
    level = block_scale(key, extent, shards, -0.22, 0.18) if shards else 1.0
    values = jax.random.normal(key, extent, jnp.float32) * deviation * level
    return jnp.minimum(jnp.maximum(values, -bound), bound).astype(kind)


def setup_inputs(seed: int = 0) -> dict:
    key_list = jax.random.split(jax.random.key(seed), 11)
    return {
        "q_clean": draw_q_clean(jax.random.fold_in(key_list[10], 71), 0),
        "k_clean": draw_k_clean(jax.random.fold_in(key_list[10], 71), 0),
        "v_clean": centred(key_list[2], (SEQ, KVH * HD), 1.0, 6.0, ((0, 256),)),
        "q_noised": draw_q_noised(jax.random.fold_in(key_list[10], 71), 0),
        "masked": with_ends((jax.random.randint(key_list[4], (SEQ,), 0, 2) < 1).astype(jnp.int32), jax.random.fold_in(key_list[4], 1), 0, 1),
        "noise_level": with_ends(jax.random.randint(key_list[5], (SEQ // BLOCK,), 0, LEVELS), jax.random.fold_in(key_list[5], 1), 0, LEVELS - 1).astype(jnp.int32),
        "mask_key": centred(key_list[6], (LEVELS, KVH * HD), 1.0, 6.0, ((1, 8),)),
        "mask_value": centred(key_list[7], (LEVELS, KVH * HD), 1.0, 6.0, ((1, 8),)),
        "d_clean": centred(key_list[8], (SEQ, QH * HD), 1.0, 6.0, ((0, 256),)),
        "d_noised": centred(key_list[9], (SEQ, QH * HD), 1.0, 6.0, ((0, 256),)),
    }


def blockwise(first_arr, second_arr):
    return jnp.einsum("bid,bjd->bij", first_arr.astype(jnp.float32), second_arr.astype(jnp.float32))


def head_pass(per_head):
    query_clean, query_noised, grad_clean, grad_noised, key_clean, value_clean, key_noised, value_noised = per_head
    scaling = 1.0 / (HD ** 0.5)
    blocks = SEQ // BLOCK
    block_ids = jnp.arange(SEQ, dtype=jnp.int32) // BLOCK
    see_clean = block_ids[None, :] <= block_ids[:, None]
    see_prior = block_ids[None, :] < block_ids[:, None]

    clean_scores = jnp.where(see_clean, jnp.dot(query_clean, key_clean.T, preferred_element_type=jnp.float32) * scaling, -jnp.inf)
    clean_weights = jax.nn.softmax(clean_scores, axis=-1)
    clean_rounded = clean_weights.astype(jnp.bfloat16)
    clean_out = jnp.dot(clean_rounded, value_clean, preferred_element_type=jnp.float32)
    clean_wgrad = jnp.dot(grad_clean, value_clean.T, preferred_element_type=jnp.float32)
    clean_terms = jnp.sum(grad_clean.astype(jnp.float32) * clean_out, axis=-1)
    clean_sgrad = (clean_weights * (clean_wgrad - clean_terms[:, None]) * scaling).astype(jnp.bfloat16)
    dq_clean_head = jnp.dot(clean_sgrad, key_clean, preferred_element_type=jnp.float32)
    dk_head = jnp.dot(clean_sgrad.T, query_clean, preferred_element_type=jnp.float32)
    dv_head = jnp.dot(clean_rounded.T, grad_clean, preferred_element_type=jnp.float32)

    query_blocks = query_noised.reshape(blocks, BLOCK, HD)
    key_blocks = key_noised.reshape(blocks, BLOCK, HD)
    value_blocks = value_noised.reshape(blocks, BLOCK, HD)
    grad_blocks = grad_noised.reshape(blocks, BLOCK, HD)
    prior_scores = jnp.where(see_prior, jnp.dot(query_noised, key_clean.T, preferred_element_type=jnp.float32) * scaling, -jnp.inf)
    self_scores = blockwise(query_blocks, key_blocks).reshape(SEQ, BLOCK) * scaling
    noised_weights = jax.nn.softmax(jnp.concatenate([prior_scores, self_scores], axis=1), axis=-1)
    prior_weights = noised_weights[:, :SEQ]
    self_weights = noised_weights[:, SEQ:]
    prior_rounded = prior_weights.astype(jnp.bfloat16)
    self_rounded = self_weights.astype(jnp.bfloat16).reshape(blocks, BLOCK, BLOCK)
    noised_out = jnp.dot(prior_rounded, value_clean, preferred_element_type=jnp.float32)
    noised_out = noised_out + jnp.einsum("bij,bjd->bid", self_rounded.astype(jnp.float32), value_blocks.astype(jnp.float32)).reshape(SEQ, HD)
    prior_wgrad = jnp.dot(grad_noised, value_clean.T, preferred_element_type=jnp.float32)
    self_wgrad = blockwise(grad_blocks, value_blocks).reshape(SEQ, BLOCK)
    noised_terms = jnp.sum(grad_noised.astype(jnp.float32) * noised_out, axis=-1)
    prior_sgrad = (prior_weights * (prior_wgrad - noised_terms[:, None]) * scaling).astype(jnp.bfloat16)
    self_sgrad = (self_weights * (self_wgrad - noised_terms[:, None]) * scaling).astype(jnp.bfloat16).reshape(blocks, BLOCK, BLOCK)
    dq_noised_head = jnp.dot(prior_sgrad, key_clean, preferred_element_type=jnp.float32)
    dq_noised_head = dq_noised_head + jnp.einsum("bij,bjd->bid", self_sgrad.astype(jnp.float32), key_blocks.astype(jnp.float32)).reshape(SEQ, HD)
    dk_head = dk_head + jnp.dot(prior_sgrad.T, query_noised, preferred_element_type=jnp.float32)
    dv_head = dv_head + jnp.dot(prior_rounded.T, grad_noised, preferred_element_type=jnp.float32)
    dk_self = jnp.einsum("bij,bid->bjd", self_sgrad.astype(jnp.float32), query_blocks.astype(jnp.float32)).reshape(SEQ, HD)
    dv_self = jnp.einsum("bij,bid->bjd", self_rounded.astype(jnp.float32), grad_blocks.astype(jnp.float32)).reshape(SEQ, HD)
    return (clean_out, noised_out, dq_clean_head, dq_noised_head, dk_head, dv_head, dk_self, dv_self)


def by_head(matrix, heads):
    return jnp.transpose(matrix.reshape(SEQ, heads, HD), (1, 0, 2))


def to_rows(stacked):
    return jnp.transpose(stacked, (1, 0, 2)).reshape(SEQ, -1)


def reference(q_clean, k_clean, v_clean, q_noised, masked, noise_level, mask_key, mask_value, d_clean, d_noised):
    group_size = QH // KVH
    level_rows = jnp.repeat(noise_level, BLOCK)
    covered = (masked == 1)[:, None]
    key_noised = jnp.where(covered, mask_key[level_rows], k_clean)
    value_noised = jnp.where(covered, mask_value[level_rows], v_clean)
    kv_index = jnp.arange(QH, dtype=jnp.int32) // group_size
    per_head = (by_head(q_clean, QH), by_head(q_noised, QH), by_head(d_clean, QH), by_head(d_noised, QH),
                by_head(k_clean, KVH)[kv_index], by_head(v_clean, KVH)[kv_index],
                by_head(key_noised, KVH)[kv_index], by_head(value_noised, KVH)[kv_index])
    clean_out, noised_out, dq_c, dq_n, dk_c, dv_c, dk_n, dv_n = lax.map(head_pass, per_head)
    kept_rows = (masked == 0)[None, :, None]
    dk_total = (dk_c + jnp.where(kept_rows, dk_n, 0.0)).reshape(KVH, group_size, SEQ, HD).sum(axis=1)
    dv_total = (dv_c + jnp.where(kept_rows, dv_n, 0.0)).reshape(KVH, group_size, SEQ, HD).sum(axis=1)
    return (to_rows(clean_out).astype(jnp.bfloat16), to_rows(noised_out).astype(jnp.bfloat16),
            to_rows(dq_c).astype(jnp.bfloat16), to_rows(dq_n).astype(jnp.bfloat16),
            to_rows(dk_total).astype(jnp.bfloat16), to_rows(dv_total).astype(jnp.bfloat16))
```

```python
import functools
import math

import jax
import jax.numpy as jnp
from jax import lax
from jax.experimental import pallas as pl
from jax.experimental.pallas import tpu as pltpu
from jax.sharding import PartitionSpec as P
bf=jnp.bfloat16; f32=jnp.float32
HD=128; BLOCK=32; T=256; C=256; G=4
NEG=-1e30
SC=1.0/math.sqrt(HD); C2=math.log2(math.e)*SC

def dot(a,b): return jnp.dot(a,b,preferred_element_type=f32)

def kernel(c_ref, qd_ref, kv_ref, nkv_ref, keep_ref, o_ref, dkv_ref, qt, dot_t, ot, dqt, ml, *, TT, CC):
    c=c_ref[0]
    nt=2048//T
    for t in range(nt):
        q=qd_ref[:, t*128:(t+1)*128].astype(f32)
        d=qd_ref[:, 1024+t*128:1024+(t+1)*128].astype(f32)
        qs=q.T*C2
        hi=qs.astype(bf)
        qt[0:128, t*T:(t+1)*T]=hi
        qt[128:256, t*T:(t+1)*T]=(qs-hi.astype(f32)).astype(bf)
        dot_t[0:128, t*T:(t+1)*T]=d.T.astype(bf)
    kb=lax.broadcasted_iota(jnp.int32,(C,T),0)//BLOCK
    qb=lax.broadcasted_iota(jnp.int32,(C,T),1)//BLOCK
    def first(kk, vt, t, mask):
        s=jnp.where(mask, dot(kk, qt[:, t*T:(t+1)*T]), NEG)
        m=jnp.max(s,axis=0,keepdims=True)
        p=jnp.exp2(s-m)
        ml[0:1, t*T:(t+1)*T]=m
        ml[1:2, t*T:(t+1)*T]=jnp.sum(p,axis=0,keepdims=True)
        ot[:, t*T:(t+1)*T]=dot(vt,p.astype(bf))
    def step(kk, vt, lo, width, mask=None):
        sl=slice(lo,lo+width)
        s=dot(kk, qt[:, sl])
        if mask is not None: s=jnp.where(mask,s,NEG)
        mo=ml[0:1, sl]
        m=jnp.maximum(mo,jnp.max(s,axis=0,keepdims=True))
        p=jnp.exp2(s-m)
        a=jnp.exp2(mo-m)
        ml[0:1, sl]=m
        ml[1:2, sl]=ml[1:2, sl]*a+jnp.sum(p,axis=0,keepdims=True)
        ot[:, sl]=ot[:, sl]*a+dot(vt,p.astype(bf))
    own=pl.ds(pl.multiple_of(c*C,C),C)
    k_own=kv_ref[own,0:128]; v_own=kv_ref[own,128:256]
    kk=jnp.concatenate([k_own,k_own],axis=1)
    vt=v_own.astype(f32).T.astype(bf)
    nk=nkv_ref[:,0:128]; nv=nkv_ref[:,128:256]
    nkk=jnp.concatenate([nk,nk],axis=1); nvt=nv.astype(f32).T.astype(bf)
    for t in range(nt//2):
        first(kk,vt,t,kb<=qb)
    for t in range(nt//2,nt):
        first(nkk,nvt,t,kb==qb)
    for t in range(nt//2,nt):
        step(kk,vt,t*T,T,kb<qb)
    def body(j,_):
        sl=pl.ds(pl.multiple_of(j*CC,CC),CC)
        k=kv_ref[sl,0:128]; v=kv_ref[sl,128:256]
        kk=jnp.concatenate([k,k],axis=1); vt=v.astype(f32).T.astype(bf)
        for t in range(2048//TT):
            step(kk,vt,t*TT,TT)
        return 0
    nfull=c*(C//CC) if CC<=C else c
    lax.fori_loop(0,nfull,body,0)
    l=ml[1:2,:]
    ml[0:1,:]=ml[0:1,:]+jnp.log2(l)
    rl=1.0/l
    dot_t[128:256,:]=jnp.zeros((128,2048),bf)
    for t in range(nt):
        sl=slice(t*T,(t+1)*T)
        o=ot[:,sl]*rl[:,sl]
        D=-jnp.sum(o*dot_t[0:128,sl].astype(f32),axis=0,keepdims=True)
        hi=D.astype(bf).astype(f32); r=D-hi
        mid=r.astype(bf).astype(f32); lo=r-mid
        row=lax.broadcasted_iota(jnp.int32,(16,T),0)
        blk=jnp.where(row==0,hi,jnp.where(row==1,mid,jnp.where(row==2,lo,0.0)))
        dot_t[128:144,sl]=blk.astype(bf)
        o_ref[:, t*128:(t+1)*128]=o.T.astype(bf)
    dqt[...]=jnp.zeros_like(dqt)
    ones=jnp.ones((C,128),bf)
    def grads(kk,kt,va,lo,width,mask=None):
        sl=slice(lo,lo+width)
        s=dot(kk,qt[:,sl])
        if mask is not None: s=jnp.where(mask,s,NEG)
        p=jnp.exp2(s-ml[0:1,sl])
        dp=dot(va,dot_t[:,sl])
        ds=(p*dp).astype(bf)
        pb=p.astype(bf)
        dqt[:,sl]=dqt[:,sl]+dot(kt,ds)
        tiles=range(lo//T,(lo+width)//T)
        qr=jnp.concatenate([qd_ref[:, t*128:(t+1)*128] for t in tiles],axis=0)
        dr=jnp.concatenate([qd_ref[:, 1024+t*128:1024+(t+1)*128] for t in tiles],axis=0)
        return dot(ds,qr), dot(pb,dr)
    def prep(k,v):
        n=k.shape[0]
        return jnp.concatenate([k,k],axis=1), k.astype(f32).T.astype(bf), jnp.concatenate([v,jnp.ones((n,128),bf)],axis=1)
    kk,kt,va=prep(k_own,v_own)
    dk=jnp.zeros((C,128),f32); dv=jnp.zeros((C,128),f32)
    for t in range(nt):
        a,b=grads(kk,kt,va,t*T,T,(kb<=qb) if t<nt//2 else (kb<qb))
        dk=dk+a; dv=dv+b
    nkk,nkt,nva=prep(nk,nv)
    sk=jnp.zeros((C,128),f32); sv=jnp.zeros((C,128),f32)
    for t in range(nt//2,nt):
        a,b=grads(nkk,nkt,nva,t*T,T,kb==qb)
        sk=sk+a; sv=sv+b
    keep=keep_ref[...]
    dk=dk+sk*keep; dv=dv+sv*keep
    dkv_ref[own,0:128]=(dk*SC).astype(bf)
    dkv_ref[own,128:256]=dv.astype(bf)
    def bbody(j,_):
        sl=pl.ds(pl.multiple_of(j*CC,CC),CC)
        kk,kt,va=prep(kv_ref[sl,0:128],kv_ref[sl,128:256])
        dk=dv=None
        for t in range(2048//TT):
            a,b=grads(kk,kt,va,t*TT,TT)
            dk=a if dk is None else dk+a; dv=b if dv is None else dv+b
        dkv_ref[sl,0:128]=(dk*SC).astype(bf)
        dkv_ref[sl,128:256]=dv.astype(bf)
        return 0
    lax.fori_loop(0,nfull,bbody,0)
    def zbody(j,_):
        sl=pl.ds(pl.multiple_of(j*C,C),C)
        dkv_ref[sl,:]=jnp.zeros((C,256),bf)
        return 0
    lax.fori_loop(c+1,32,zbody,0)
    for t in range(nt):
        o_ref[:, 1024+t*128:1024+(t+1)*128]=(dqt[:, t*T:(t+1)*T]*SC).T.astype(bf)


def attend(c, qd, kv, nkv, keep):
    vm = pl.BlockSpec(memory_space=pltpu.VMEM)
    return pl.pallas_call(
        functools.partial(kernel, TT=512, CC=256),
        out_shape=(jax.ShapeDtypeStruct((256, 2048), bf), jax.ShapeDtypeStruct((8192, 256), bf)),
        in_specs=[pl.BlockSpec(memory_space=pltpu.SMEM), vm, vm, vm, vm],
        out_specs=(vm, vm),
        scratch_shapes=[
            pltpu.VMEM((256, 2048), bf),
            pltpu.VMEM((256, 2048), bf),
            pltpu.VMEM((128, 2048), f32),
            pltpu.VMEM((128, 2048), f32),
            pltpu.VMEM((8, 2048), f32),
        ],
        compiler_params=pltpu.CompilerParams(vmem_limit_bytes=48 * 1024 * 1024),
        cost_estimate=pl.CostEstimate(flops=60_000_000_000, bytes_accessed=12_000_000, transcendentals=30_000_000),
        name="attend",
    )(c, qd, kv, nkv, keep)


X_GROUPS = [[x * 8 + z for x in range(4)] for z in range(8)]
Z_GROUPS = [[x * 8 + z for z in range(8)] for x in range(4)]
LEVELS = 8


def to_heads(parts):
    cut = [p.reshape(32, 8, -1) for p in parts]
    sent = jnp.transpose(jnp.concatenate(cut, axis=2), (1, 0, 2))
    got = lax.all_to_all(sent, "head", split_axis=0, concat_axis=0, tiled=True)
    return got.reshape(256, -1)


def to_tokens(rows, parts):
    got = lax.all_to_all(rows.reshape(8, 32, -1), "head", split_axis=0, concat_axis=0, tiled=True)
    got = jnp.transpose(got, (1, 0, 2)).reshape(32, 8, parts, -1)
    return tuple(got[:, :, i].reshape(32, -1) for i in range(parts))


def on_device(q_clean, k_clean, v_clean, q_noised, masked, noise_level, mask_key, mask_value, d_clean, d_noised):
    kv = to_heads((k_clean, v_clean))
    kv_all = lax.all_gather(kv, "ctx", axis=0, tiled=True)
    qd = to_heads((q_clean, q_noised, d_clean, d_noised))
    onehot = (noise_level[:, None] == jnp.arange(LEVELS, dtype=jnp.int32)[None, :]).astype(bf)
    table = jnp.dot(onehot, jnp.concatenate([mask_key, mask_value], axis=1), preferred_element_type=f32).astype(bf)
    table = jnp.repeat(table, BLOCK, axis=0)
    nkv = jnp.where((masked == 1)[:, None], table, kv)
    keep = jnp.broadcast_to((masked == 0).astype(f32)[:, None], (256, 128))
    c = lax.axis_index("ctx").reshape(1)
    rows, dkv = attend(c, qd, kv_all, nkv, keep)
    dkv = lax.psum_scatter(dkv, "ctx", scatter_dimension=0, tiled=True, axis_index_groups=X_GROUPS)
    dkv = lax.psum_scatter(dkv, "ctx", scatter_dimension=0, tiled=True, axis_index_groups=Z_GROUPS)
    return to_tokens(rows, 4) + to_tokens(dkv, 2)


def solution(mesh):
    tokens = P(("ctx", "head"), None)
    return jax.shard_map(
        on_device,
        mesh=mesh,
        in_specs=(tokens,) * 4 + (P("ctx"), P("ctx"), P(None, "head"), P(None, "head"), tokens, tokens),
        out_specs=(tokens,) * 6,
        check_vma=False,
    )
```

```python
import functools
import math

import jax
import jax.numpy as jnp
from jax import lax
from jax.experimental import pallas as pl
from jax.experimental.pallas import tpu as pltpu
from jax.sharding import PartitionSpec as P

bf = jnp.bfloat16
f32 = jnp.float32
BLOCK = 32
LEVELS = 8
NX, NZ, NH = 4, 8, 8
C = 256
W = 1024
NEG = -1e30
SC = 1.0 / math.sqrt(128)
C2 = math.log2(math.e) * SC


def dot(a, b):
    return jnp.dot(a, b, preferred_element_type=f32)


def cols(part, stream):
    return slice(part * W + stream * 512, part * W + stream * 512 + 512)


def masks():
    key_block = lax.broadcasted_iota(jnp.int32, (C, 512), 0) // BLOCK
    row_block = (lax.broadcasted_iota(jnp.int32, (C, 512), 1) % 128) // 16
    return key_block, row_block


def twice(k):
    return jnp.concatenate([k, k], axis=1)


def flip(a):
    return a.astype(f32).T.astype(bf)


def fold(kv, qt, ml, ot, sl, mask=None):
    s = dot(twice(kv[:, 0:128]), qt[:, sl])
    if mask is not None:
        s = jnp.where(mask, s, NEG)
    old = ml[0:1, sl]
    m = jnp.maximum(old, jnp.max(s, axis=0, keepdims=True))
    p = jnp.exp2(s - m)
    a = jnp.exp2(old - m)
    ml[0:1, sl] = m
    ml[1:2, sl] = ml[1:2, sl] * a + jnp.sum(p, axis=0, keepdims=True)
    ot[:, sl] = ot[:, sl] * a + dot(flip(kv[:, 128:256]), p.astype(bf))


def first(kv, qt, ml, ot, sl, mask):
    s = jnp.where(mask, dot(twice(kv[:, 0:128]), qt[:, sl]), NEG)
    m = jnp.max(s, axis=0, keepdims=True)
    p = jnp.exp2(s - m)
    ml[0:1, sl] = m
    ml[1:2, sl] = jnp.sum(p, axis=0, keepdims=True)
    ot[:, sl] = dot(flip(kv[:, 128:256]), p.astype(bf))


def group_bounds(sc_ref, offset):
    z = sc_ref[2]
    earlier = (lax.rem(z + offset, NZ) < z).astype(jnp.int32)
    return sc_ref[0] + earlier, sc_ref[1] + earlier


def fold_group(sc_ref, offset, kv_ref, qt, ml, ot):
    low, high = group_bounds(sc_ref, offset)

    def both(i, _):
        fold(kv_ref[i], qt, ml, ot, slice(0, 2 * W))
        return 0

    def one(i, _):
        fold(kv_ref[i], qt, ml, ot, slice(W, 2 * W))
        return 0

    lax.fori_loop(0, low, both, 0)
    lax.fori_loop(low, high, one, 0)


def begin_kernel(sc_ref, qd_ref, kv_ref, nkv_ref, qt, dt, rows, ml, ot):
    for part in range(2):
        for t in range(8):
            at = part * W + t * 128
            q = qd_ref[part * 128 : part * 128 + 128, t * 128 : t * 128 + 128]
            d = qd_ref[part * 128 : part * 128 + 128, 1024 + t * 128 : 1024 + t * 128 + 128]
            rows[at : at + 128, 0:128] = q
            rows[at : at + 128, 128:256] = d
            qs = q.astype(f32).T * C2
            upper = qs.astype(bf)
            qt[0:128, at : at + 128] = upper
            qt[128:256, at : at + 128] = (qs - upper.astype(f32)).astype(bf)
            dt[0:128, at : at + 128] = flip(d)
    ml[...] = jnp.zeros_like(ml)
    kb, rb = masks()
    for part in range(2):
        own = kv_ref[sc_ref[part]]
        first(own, qt, ml, ot, cols(part, 0), kb <= rb)
        first(nkv_ref[part], qt, ml, ot, cols(part, 1), kb == rb)
        fold(own, qt, ml, ot, cols(part, 1), kb < rb)
    fold_group(sc_ref, 0, kv_ref, qt, ml, ot)


def more_kernel(offsets, sc_ref, qt, ml_in, ot_in, *refs):
    kvs, (ml, ot) = refs[: len(offsets)], refs[len(offsets) :]
    ml[...] = ml_in[...]
    ot[...] = ot_in[...]
    for offset, kv_ref in zip(offsets, kvs):
        fold_group(sc_ref, offset, kv_ref, qt, ml, ot)


def last_kernel(sc_ref, qt, dt_in, ml_in, ot_in, ka_ref, kb_ref, ml, dt, o_ref, ot, kv):
    ml[...] = ml_in[...]
    ot[...] = ot_in[...]
    kv[0:2] = ka_ref[...]
    kv[2:4] = kb_ref[...]
    fold_group(sc_ref, 4, kv, qt, ml, ot)
    total = ml[1:2, :]
    inverse = 1.0 / total
    ml[0:1, :] = ml[0:1, :] + jnp.log2(total)
    dt[0:128, :] = dt_in[0:128, :]
    dt[128:256, :] = jnp.zeros((128, 2 * W), bf)
    row = lax.broadcasted_iota(jnp.int32, (16, 128), 0)
    for part in range(2):
        for t in range(8):
            sl = slice(part * W + t * 128, part * W + t * 128 + 128)
            o = ot[:, sl] * inverse[:, sl]
            term = -jnp.sum(o * dt_in[0:128, sl].astype(f32), axis=0, keepdims=True)
            a = term.astype(bf).astype(f32)
            b = (term - a).astype(bf).astype(f32)
            c = term - a - b
            dt[128:144, sl] = jnp.where(row == 0, a, jnp.where(row == 1, b, jnp.where(row == 2, c, 0.0))).astype(bf)
            o_ref[part * 128 : part * 128 + 128, t * 128 : t * 128 + 128] = o.T.astype(bf)


def grads(kv, qt, dt, rows, ml, dq, sl, mask=None):
    k = kv[:, 0:128]
    s = dot(twice(k), qt[:, sl])
    if mask is not None:
        s = jnp.where(mask, s, NEG)
    p = jnp.exp2(s - ml[0:1, sl])
    dp = dot(jnp.concatenate([kv[:, 128:256], jnp.ones((C, 128), bf)], axis=1), dt[:, sl])
    ds = (p * dp).astype(bf)
    dq[:, sl] = dq[:, sl] + dot(flip(k), ds)
    return dot(ds, rows[sl, 0:128]), dot(p.astype(bf), rows[sl, 128:256])


def grad_group(sc_ref, offset, kv_ref, qt, dt, rows, ml, dq, out):
    low, high = group_bounds(sc_ref, offset)

    def put(i, dk, dv):
        out[i, :, 0:128] = (dk * SC).astype(out.dtype)
        out[i, :, 128:256] = dv.astype(out.dtype)

    def both(i, _):
        put(i, *grads(kv_ref[i], qt, dt, rows, ml, dq, slice(0, 2 * W)))
        return 0

    def one(i, _):
        put(i, *grads(kv_ref[i], qt, dt, rows, ml, dq, slice(W, 2 * W)))
        return 0

    def none(i, _):
        out[i] = jnp.zeros((C, 256), out.dtype)
        return 0

    lax.fori_loop(0, low, both, 0)
    lax.fori_loop(low, high, one, 0)
    lax.fori_loop(high, NX, none, 0)


def far_kernel(sc_ref, qt, dt, rows, ml, ka_ref, kb_ref, dq, oa, ob, kv, out):
    dq[...] = jnp.zeros_like(dq)
    kv[0:2] = ka_ref[...]
    kv[2:4] = kb_ref[...]
    grad_group(sc_ref, 4, kv, qt, dt, rows, ml, dq, out)
    oa[...] = out[0:2]
    ob[...] = out[2:4]


def pair_kernel(offsets, sc_ref, qt, dt, rows, ml, dq_in, ka_ref, kb_ref, dq, oa, ob):
    dq[...] = dq_in[...]
    grad_group(sc_ref, offsets[0], ka_ref, qt, dt, rows, ml, dq, oa)
    grad_group(sc_ref, offsets[1], kb_ref, qt, dt, rows, ml, dq, ob)


def own_kernel(sc_ref, qt, dt, rows, ml, dq_in, kv_ref, nkv_ref, keep_ref, dq_rows, out, dq, acc):
    dq[...] = dq_in[...]
    grad_group(sc_ref, 0, kv_ref, qt, dt, rows, ml, dq, acc)
    kb, rb = masks()
    for part in range(2):
        i = sc_ref[part]
        own = kv_ref[i]
        ka, va = grads(own, qt, dt, rows, ml, dq, cols(part, 0), kb <= rb)
        kc, vc = grads(own, qt, dt, rows, ml, dq, cols(part, 1), kb < rb)
        ks, vs = grads(nkv_ref[part], qt, dt, rows, ml, dq, cols(part, 1), kb == rb)
        keep = keep_ref[part]
        acc[i, :, 0:128] += (ka + kc + ks * keep) * SC
        acc[i, :, 128:256] += va + vc + vs * keep
    out[...] = acc[...].astype(bf)
    for part in range(2):
        for t in range(8):
            sl = slice(part * W + t * 128, part * W + t * 128 + 128)
            dq_rows[part * 128 : part * 128 + 128, t * 128 : t * 128 + 128] = (dq[:, sl] * SC).T.astype(bf)


def call(body, name, outs, args, scratch=(), work=1):
    vm = pl.BlockSpec(memory_space=pltpu.VMEM)
    return pl.pallas_call(
        body,
        out_shape=tuple(jax.ShapeDtypeStruct(*o) for o in outs),
        in_specs=[pl.BlockSpec(memory_space=pltpu.SMEM)] + [vm] * (len(args) - 1),
        out_specs=(vm,) * len(outs),
        scratch_shapes=[pltpu.VMEM(*s) for s in scratch],
        compiler_params=pltpu.CompilerParams(vmem_limit_bytes=32 * 1024 * 1024),
        cost_estimate=pl.CostEstimate(flops=work * 1_000_000_000, bytes_accessed=4_000_000, transcendentals=work * 500_000),
        name=name,
    )(*args)


def device(x, z, h):
    return (x * NZ + z) * NH + h


BOTH = ("ctx", "head")
PLANE = [[device(x, z, h) for x in range(NX) for h in range(NH)] for z in range(NZ)]
MIRROR = [[device(x, z, h) for x in (a, NX - 1 - a) for h in range(NH)] for z in range(NZ) for a in range(2)]
UP = [(x * NZ + z, x * NZ + (z + 1) % NZ) for x in range(NX) for z in range(NZ)]
DOWN = [(x * NZ + z, x * NZ + (z - 1) % NZ) for x in range(NX) for z in range(NZ)]
SWAP = [(x * NZ + z, (NX - 1 - x) * NZ + z) for x in range(NX) for z in range(NZ)]


def exchange(a, groups):
    return lax.all_to_all(a, BOTH, split_axis=0, concat_axis=0, tiled=True, axis_index_groups=groups)


def up(a):
    return lax.ppermute(a, "ctx", UP)


def down(a):
    return lax.ppermute(a, "ctx", DOWN)


def spread(parts):
    cut = [jnp.transpose(p.reshape(2, 16, NH, 512), (0, 2, 1, 3)) for p in parts]
    sent = jnp.concatenate(cut, axis=3).reshape(16, 16, -1)
    return exchange(sent, MIRROR).reshape(256, -1)


def collect(rows, parts):
    got = exchange(rows.reshape(16, 16, -1), MIRROR).reshape(2, NH, 16, parts, 512)
    return tuple(jnp.transpose(got[:, :, :, i], (0, 2, 1, 3)).reshape(32, -1) for i in range(parts))


def on_device(q_clean, k_clean, v_clean, q_noised, masked, noise_level, mask_key, mask_value, d_clean, d_noised):
    ctx = lax.axis_index("ctx")
    x, z = ctx // NZ, ctx % NZ
    lo = jnp.minimum(x, NX - 1 - x)
    sc = jnp.stack([lo, NX - 1 - lo, z]).astype(jnp.int32)

    kv = jnp.concatenate([k_clean.reshape(32, NH, 128), v_clean.reshape(32, NH, 128)], axis=2)
    kv = jnp.broadcast_to(jnp.transpose(kv, (1, 0, 2))[None], (NX, NH, 32, 256)).reshape(NX * NH, 32, 256)
    here = exchange(kv, PLANE).reshape(NX, C, 256)
    qd = spread((q_clean, q_noised, d_clean, d_noised))
    info = jnp.concatenate([masked, noise_level])
    other = lax.ppermute(info, "ctx", SWAP)
    info = jnp.where(x < 2, jnp.stack([info, other]), jnp.stack([other, info]))
    covered = info[:, :C] == 1
    onehot = (info[:, C:, None] == jnp.arange(LEVELS, dtype=jnp.int32)).astype(bf)
    table = dot(onehot.reshape(16, LEVELS), jnp.concatenate([mask_key, mask_value], axis=1)).astype(bf)
    table = jnp.repeat(table, BLOCK, axis=0).reshape(2, C, 256)
    mine = jnp.stack([lax.dynamic_index_in_dim(here, sc[i], 0, keepdims=False) for i in range(2)])
    nkv = jnp.where(covered[:, :, None], table, mine)
    keep = jnp.broadcast_to((info[:, :C] == 0).astype(f32)[:, :, None], (2, C, 128))

    a1, b1 = up(here), down(here)
    a2, b2 = up(a1), down(b1)
    a3, b3 = up(a2), down(b2)
    a4, b4 = up(a3[0:2]), down(b3[2:4])

    state = [((8, 2 * W), f32), ((128, 2 * W), f32)]
    square = ((256, 2 * W), bf)
    part = ((NX, C, 256), bf)
    half = ((2, C, 256), bf)
    qt, dt, rows, ml, ot = call(
        begin_kernel, "begin", [square, ((128, 2 * W), bf), ((2 * W, 256), bf)] + state, (sc, qd, here, nkv), work=5
    )
    for name, offsets, pair in (("near", (7, 1), (a1, b1)), ("second", (6, 2), (a2, b2)), ("third", (5, 3), (a3, b3))):
        ml, ot = call(functools.partial(more_kernel, offsets), name, state, (sc, qt, ml, ot) + pair, work=4)
    ml, dt, o_rows = call(
        last_kernel, "finish", [state[0], square, ((256, 1024), bf)], (sc, qt, dt, ml, ot, a4, b4), [state[1], part], work=3
    )
    fixed = (sc, qt, dt, rows, ml)
    dq_state = ((128, 2 * W), f32)
    dq, ga, gb = call(far_kernel, "back4", [dq_state, half, half], fixed + (a4, b4), [part, part], work=4)
    ga, gb = up(ga), down(gb)
    dq, pa, pb = call(functools.partial(pair_kernel, (3, 5)), "back3", [dq_state, part, part], fixed + (dq, b3, a3), work=7)
    ga = jnp.concatenate([pa[0:2] + ga, pa[2:4]], axis=0)
    gb = jnp.concatenate([pb[0:2], pb[2:4] + gb], axis=0)
    dq, ga, gb = lax.optimization_barrier((dq, ga, gb))
    ga, gb = up(ga), down(gb)
    outs = collect(o_rows, 2)
    dq, pa, pb = call(functools.partial(pair_kernel, (2, 6)), "back2", [dq_state, part, part], fixed + (dq, b2, a2), work=7)
    dq, ga, gb = lax.optimization_barrier((dq, pa + ga, pb + gb))
    ga, gb = up(ga), down(gb)
    dq, pa, pb = call(functools.partial(pair_kernel, (1, 7)), "back1", [dq_state, part, part], fixed + (dq, b1, a1), work=7)
    dq, ga, gb = lax.optimization_barrier((dq, pa + ga, pb + gb))
    ga, gb = up(ga), down(gb)
    dq_rows, own = call(
        own_kernel, "back0", [((256, 1024), bf), part], fixed + (dq, here, nkv, keep), [dq_state, ((NX, C, 256), f32)], work=6
    )
    dqs = collect(dq_rows, 2)
    total = (own.astype(f32) + ga.astype(f32) + gb.astype(f32)).astype(bf)
    got = exchange(total.reshape(NX * NH, 32, 256), PLANE).reshape(NX, NH, 32, 256)
    got = jnp.sum(got.astype(f32), axis=0)
    got = jnp.transpose(got, (1, 0, 2)).astype(bf)
    return outs + dqs + (got[:, :, 0:128].reshape(32, -1), got[:, :, 128:256].reshape(32, -1))


def solution(mesh):
    tokens = P(("ctx", "head"), None)
    return jax.shard_map(
        on_device,
        mesh=mesh,
        in_specs=(tokens,) * 4 + (P("ctx"), P("ctx"), P(None, "head"), P(None, "head"), tokens, tokens),
        out_specs=(tokens,) * 6,
        check_vma=False,
    )
```

```python
import functools
import math

import jax
import jax.numpy as jnp
from jax import lax
from jax.experimental import pallas as pl
from jax.experimental.pallas import tpu as pltpu
from jax.sharding import PartitionSpec as P

bf = jnp.bfloat16
f32 = jnp.float32
BLOCK = 32
LEVELS = 8
NX, NZ, NH = 4, 8, 8
C = 256
W = 1024
NEG = -1e30
SC = 1.0 / math.sqrt(128)
C2 = math.log2(math.e) * SC


def dot(a, b):
    return jnp.dot(a, b, preferred_element_type=f32)


def flip(a):
    return a.astype(f32).T.astype(bf)


def cols(part, stream):
    return slice(part * W + stream * 512, part * W + stream * 512 + 512)


def tiles():
    for part in range(2):
        for t in range(8):
            at = part * W + t * 128
            yield slice(at, at + 128), slice(part * 128, part * 128 + 128), slice(t * 128, t * 128 + 128)


def masks():
    key_block = lax.broadcasted_iota(jnp.int32, (C, 512), 0) // BLOCK
    row_block = (lax.broadcasted_iota(jnp.int32, (C, 512), 1) % 128) // 16
    return key_block, row_block


def chunks(j, n=1):
    return pl.ds(pl.multiple_of(j * C, C), n * C)


def group_bounds(sc_ref, offset):
    z = sc_ref[2]
    earlier = (lax.rem(z + offset, NZ) < z).astype(jnp.int32)
    return sc_ref[0] + earlier, sc_ref[1] + earlier


class Plan:
    def __init__(self, sc_ref, groups):
        self.groups = [kv_ref for _, kv_ref in groups]
        self.bounds = [group_bounds(sc_ref, offset) for offset, _ in groups]
        self.early = sum(low for low, _ in self.bounds)
        self.late = sum(high for _, high in self.bounds)

    def place(self, g, i):
        low, _ = self.bounds[g]
        low_base, high_base = 0, self.early
        if g:
            low_base = self.bounds[0][0]
            high_base = self.early + self.bounds[0][1] - self.bounds[0][0]
        return jnp.where(i < low, low_base + i, high_base + i - low)

    def each(self, body):
        for g, kv_ref in enumerate(self.groups):

            def one(i, _):
                body(self.place(g, i), kv_ref[i])
                return 0

            lax.fori_loop(0, self.bounds[g][1], one, 0)

    def sweep(self, unit):
        late, early = self.late // 2, self.early // 2

        def double(k, _):
            part = (k < late).astype(jnp.int32)
            unit(jnp.where(part == 1, k, k - late) * 2, 2, pl.ds(pl.multiple_of(part * W, W), W))
            return 0

        lax.fori_loop(0, late + early, double, 0)
        late_left, early_left = self.late - 2 * late, self.early - 2 * early

        def single(k, _):
            part = (k < late_left).astype(jnp.int32)
            unit(jnp.where(part == 1, 2 * late, 2 * early), 1, pl.ds(pl.multiple_of(part * W, W), W))
            return 0

        lax.fori_loop(0, late_left + early_left, single, 0)


def fold(kv, qt, ml, ot, sl, mask=None):
    s = dot(kv[:, 0:128], qt[:, sl]) * C2
    if mask is not None:
        s = jnp.where(mask, s, NEG)
    old = ml[0:1, sl]
    m = jnp.maximum(old, jnp.max(s, axis=0, keepdims=True))
    p = jnp.exp2(s - m)
    a = jnp.exp2(old - m)
    ml[0:1, sl] = m
    ml[1:2, sl] = ml[1:2, sl] * a + jnp.sum(p, axis=0, keepdims=True)
    ot[:, sl] = ot[:, sl] * a + dot(flip(kv[:, 128:256]), p.astype(bf))


def first(kv, qt, ml, ot, sl, mask):
    s = jnp.where(mask, dot(kv[:, 0:128], qt[:, sl]) * C2, NEG)
    m = jnp.max(s, axis=0, keepdims=True)
    p = jnp.exp2(s - m)
    ml[0:1, sl] = m
    ml[1:2, sl] = jnp.sum(p, axis=0, keepdims=True)
    ot[:, sl] = dot(flip(kv[:, 128:256]), p.astype(bf))


def fold_slow(plan, qt, ml, ot):
    for g, kv_ref in enumerate(plan.groups):
        low, high = plan.bounds[g]

        def one(k, _):
            part = (k < high).astype(jnp.int32)
            fold(kv_ref[k - (1 - part) * high], qt, ml, ot, pl.ds(pl.multiple_of(part * W, W), W))
            return 0

        lax.fori_loop(0, low + high, one, 0)


def fold_groups(sc_ref, groups, qt, ml, ot, ml_old, ot_old, ks, vs, kt, vt):
    ml[...] = ml_old[...]
    ot[...] = ot_old[...]
    plan = Plan(sc_ref, groups)

    def prepare(j, kv):
        ks[chunks(j), :] = kv[:, 0:128]
        vs[chunks(j), :] = kv[:, 128:256]
        kt[:, chunks(j)] = flip(kv[:, 0:128])
        vt[:, chunks(j)] = flip(kv[:, 128:256])

    plan.each(prepare)

    def unit(j, n, sl):
        p = jnp.exp2(dot(ks[chunks(j, n), :], qt[:, sl]) * C2 - ml[0:1, sl])
        ml[1:2, sl] = ml[1:2, sl] + jnp.sum(p, axis=0, keepdims=True)
        ot[:, sl] = ot[:, sl] + dot(vt[:, chunks(j, n)], p.astype(bf))

    plan.sweep(unit)

    @pl.when(jnp.logical_not(jnp.max(ml[1:2, :]) < 2.0**64))
    def _():
        ml[...] = ml_old[...]
        ot[...] = ot_old[...]
        fold_slow(plan, qt, ml, ot)


def begin_kernel(sc_ref, qd_ref, kv_ref, nkv_ref, qt, dt, rows, ml_out, ot_out, ks, vs, kt, vt, ml, ot):
    for sl, here, at in tiles():
        q = qd_ref[here, at]
        d = qd_ref[here, 1024 + at.start : 1024 + at.stop]
        rows[sl, 0:128] = q
        rows[sl, 128:256] = d
        qt[:, sl] = flip(q)
        dt[:, sl] = flip(d)
    ml[...] = jnp.zeros_like(ml)
    kb, rb = masks()
    for part in range(2):
        own = kv_ref[sc_ref[part]]
        first(own, qt, ml, ot, cols(part, 0), kb <= rb)
        first(nkv_ref[part], qt, ml, ot, cols(part, 1), kb == rb)
        fold(own, qt, ml, ot, cols(part, 1), kb < rb)
    fold_groups(sc_ref, [(0, kv_ref)], qt, ml_out, ot_out, ml, ot, ks, vs, kt, vt)


def more_kernel(offsets, sc_ref, qt, ml_in, ot_in, ka_ref, kb_ref, ml, ot, ks, vs, kt, vt):
    fold_groups(sc_ref, list(zip(offsets, (ka_ref, kb_ref))), qt, ml, ot, ml_in, ot_in, ks, vs, kt, vt)


def last_kernel(sc_ref, qt, dt, ml_in, ot_in, ka_ref, kb_ref, ml, o_ref, ks, vs, kt, kv, ot, vt):
    kv[0:2] = ka_ref[...]
    kv[2:4] = kb_ref[...]
    fold_groups(sc_ref, [(4, kv)], qt, ml, ot, ml_in, ot_in, ks, vs, kt, vt)
    total = ml[1:2, :]
    inverse = 1.0 / total
    ml[0:1, :] = ml[0:1, :] + jnp.log2(total)
    for sl, here, at in tiles():
        o = ot[:, sl] * inverse[:, sl]
        ml[2:3, sl] = jnp.sum(o * dt[:, sl].astype(f32), axis=0, keepdims=True)
        o_ref[here, at] = o.T.astype(bf)


def grads(k, v, kt, qt, dt, rows, ml, dq, sl, mask=None):
    s = dot(k, qt[:, sl]) * C2
    if mask is not None:
        s = jnp.where(mask, s, NEG)
    p = jnp.exp2(s - ml[0:1, sl])
    ds = (p * (dot(v, dt[:, sl]) - ml[2:3, sl])).astype(bf)
    dq[:, sl] = dq[:, sl] + dot(kt, ds)
    return dot(ds, rows[sl, 0:128]), dot(p.astype(bf), rows[sl, 128:256])


def grad_groups(sc_ref, offsets, qt, dt, rows, ml, dq, ks, vs, kt, acc):
    plan = Plan(sc_ref, [(offset, None) for offset in offsets])

    def clear(j, _):
        acc[chunks(j), :] = jnp.zeros((C, 256), f32)
        return 0

    lax.fori_loop(0, plan.late, clear, 0)

    def unit(j, n, sl):
        at = chunks(j, n)
        dk, dv = grads(ks[at, :], vs[at, :], kt[:, at], qt, dt, rows, ml, dq, sl)
        acc[at, 0:128] += dk
        acc[at, 128:256] += dv

    plan.sweep(unit)
    return plan


def hand_over(plan, acc, outs):
    for g, put in enumerate(outs):
        high = plan.bounds[g][1]

        def some(i, _):
            j = chunks(plan.place(g, i))
            put(i, jnp.concatenate([acc[j, 0:128] * SC, acc[j, 128:256]], axis=1).astype(bf))
            return 0

        def none(i, _):
            put(i, jnp.zeros((C, 256), bf))
            return 0

        lax.fori_loop(0, high, some, 0)
        lax.fori_loop(high, NX, none, 0)


def into(ref):
    def put(i, value):
        ref[i] = value

    return put


def far_kernel(sc_ref, qt, dt, rows, ml, ks, vs, kt, dq, oa, ob, acc, out):
    dq[...] = jnp.zeros_like(dq)
    plan = grad_groups(sc_ref, (4,), qt, dt, rows, ml, dq, ks, vs, kt, acc)
    hand_over(plan, acc, [into(out)])
    oa[...] = out[0:2]
    ob[...] = out[2:4]


def pair_kernel(offsets, sc_ref, qt, dt, rows, ml, dq_in, ks, vs, kt, dq, oa, ob, acc):
    dq[...] = dq_in[...]
    plan = grad_groups(sc_ref, offsets, qt, dt, rows, ml, dq, ks, vs, kt, acc)
    hand_over(plan, acc, [into(oa), into(ob)])


def own_kernel(sc_ref, qt, dt, rows, ml, dq_in, ks, vs, kt, kv_ref, nkv_ref, keep_ref, dq, out, acc):
    dq[...] = dq_in[...]
    plan = grad_groups(sc_ref, (0,), qt, dt, rows, ml, dq, ks, vs, kt, acc)
    kb, rb = masks()
    for part in range(2):
        i = sc_ref[part]
        own, noised = kv_ref[i], nkv_ref[part]
        k, v, turned = own[:, 0:128], own[:, 128:256], flip(own[:, 0:128])
        ka, va = grads(k, v, turned, qt, dt, rows, ml, dq, cols(part, 0), kb <= rb)
        kc, vc = grads(k, v, turned, qt, dt, rows, ml, dq, cols(part, 1), kb < rb)
        k, v, turned = noised[:, 0:128], noised[:, 128:256], flip(noised[:, 0:128])
        kn, vn = grads(k, v, turned, qt, dt, rows, ml, dq, cols(part, 1), kb == rb)
        keep = keep_ref[part]
        seen = i < plan.late
        before = acc[chunks(i), :]
        acc[chunks(i), 0:128] = jnp.where(seen, before[:, 0:128], 0.0) + ka + kc + kn * keep
        acc[chunks(i), 128:256] = jnp.where(seen, before[:, 128:256], 0.0) + va + vc + vn * keep
    plan.bounds = [(plan.bounds[0][0], plan.bounds[0][1] + 1)]
    hand_over(plan, acc, [into(out)])


def near_grads_kernel(sc_ref, qt, dt, rows, ml, dq_in, ks, vs, kt, dq_rows, oa, ob, dq, acc):
    pair_kernel((7, 1), sc_ref, qt, dt, rows, ml, dq_in, ks, vs, kt, dq, oa, ob, acc)
    for sl, here, at in tiles():
        dq_rows[here, at] = (dq[:, sl] * SC).T.astype(bf)


def call(body, name, outs, args, scratch):
    vm = pl.BlockSpec(memory_space=pltpu.VMEM)
    return pl.pallas_call(
        body,
        out_shape=tuple(jax.ShapeDtypeStruct(*o) for o in outs),
        in_specs=[pl.BlockSpec(memory_space=pltpu.SMEM)] + [vm] * (len(args) - 1),
        out_specs=(vm,) * len(outs),
        scratch_shapes=[pltpu.VMEM(*s) for s in scratch],
        compiler_params=pltpu.CompilerParams(vmem_limit_bytes=32 * 1024 * 1024),
        cost_estimate=pl.CostEstimate(flops=200_000_000, bytes_accessed=1_000_000, transcendentals=1_000_000),
        name=name,
    )(*args)


def device(x, z, h):
    return (x * NZ + z) * NH + h


BOTH = ("ctx", "head")
PLANE = [[device(x, z, h) for x in range(NX) for h in range(NH)] for z in range(NZ)]
MIRROR = [[device(x, z, h) for x in (a, NX - 1 - a) for h in range(NH)] for z in range(NZ) for a in range(2)]
UP = [(x * NZ + z, x * NZ + (z + 1) % NZ) for x in range(NX) for z in range(NZ)]
DOWN = [(x * NZ + z, x * NZ + (z - 1) % NZ) for x in range(NX) for z in range(NZ)]
SWAP = [(x * NZ + z, (NX - 1 - x) * NZ + z) for x in range(NX) for z in range(NZ)]


def exchange(a, groups):
    return lax.all_to_all(a, BOTH, split_axis=0, concat_axis=0, tiled=True, axis_index_groups=groups)


def up(a):
    return lax.ppermute(a, "ctx", UP)


def down(a):
    return lax.ppermute(a, "ctx", DOWN)


def spread(parts):
    cut = [jnp.transpose(p.reshape(2, 16, NH, 512), (0, 2, 1, 3)) for p in parts]
    sent = jnp.concatenate(cut, axis=3).reshape(16, 16, -1)
    return exchange(sent, MIRROR).reshape(256, -1)


def collect(rows, parts):
    got = exchange(rows.reshape(16, 16, -1), MIRROR).reshape(2, NH, 16, parts, 512)
    return tuple(jnp.transpose(got[:, :, :, i], (0, 2, 1, 3)).reshape(32, -1) for i in range(parts))


def on_device(q_clean, k_clean, v_clean, q_noised, masked, noise_level, mask_key, mask_value, d_clean, d_noised):
    ctx = lax.axis_index("ctx")
    x, z = ctx // NZ, ctx % NZ
    lo = jnp.minimum(x, NX - 1 - x)
    sc = jnp.stack([lo, NX - 1 - lo, z]).astype(jnp.int32)

    kv = jnp.concatenate([k_clean.reshape(32, NH, 128), v_clean.reshape(32, NH, 128)], axis=2)
    kv = jnp.broadcast_to(jnp.transpose(kv, (1, 0, 2))[None], (NX, NH, 32, 256)).reshape(NX * NH, 32, 256)
    here = exchange(kv, PLANE).reshape(NX, C, 256)
    qd = spread((q_clean, q_noised, d_clean, d_noised))
    info = jnp.concatenate([masked, noise_level])
    other = lax.ppermute(info, "ctx", SWAP)
    info = jnp.where(x < 2, jnp.stack([info, other]), jnp.stack([other, info]))
    covered = info[:, :C] == 1
    onehot = (info[:, C:, None] == jnp.arange(LEVELS, dtype=jnp.int32)).astype(bf)
    table = dot(onehot.reshape(16, LEVELS), jnp.concatenate([mask_key, mask_value], axis=1)).astype(bf)
    table = jnp.repeat(table, BLOCK, axis=0).reshape(2, C, 256)
    mine = jnp.stack([lax.dynamic_index_in_dim(here, sc[i], 0, keepdims=False) for i in range(2)])
    nkv = jnp.where(covered[:, :, None], table, mine)
    keep = jnp.broadcast_to((info[:, :C] == 0).astype(f32)[:, :, None], (2, C, 128))

    a1, b1 = up(here), down(here)
    a2, b2 = up(a1), down(b1)
    state = [((8, 2 * W), f32), ((128, 2 * W), f32)]
    turned = ((128, 2 * W), bf)
    part = ((NX, C, 256), bf)
    half = ((2, C, 256), bf)
    keys = [((8 * C, 128), bf), ((8 * C, 128), bf), ((128, 8 * C), bf)]
    values = [((128, 8 * C), bf)]
    acc = [((8 * C, 256), f32)]
    qt, dt, rows, ml, ot, *keys0 = call(
        begin_kernel, "begin", [turned, turned, ((2 * W, 256), bf)] + state + keys, (sc, qd, here, nkv), values + state
    )
    a2, b2, ml = lax.optimization_barrier((a2, b2, ml))
    a3, b3 = up(a2), down(b2)
    ml, ot, *keys1 = call(functools.partial(more_kernel, (7, 1)), "near", state + keys, (sc, qt, ml, ot, a1, b1), values)
    ml, ot, *keys2 = call(functools.partial(more_kernel, (6, 2)), "second", state + keys, (sc, qt, ml, ot, a2, b2), values)
    a3, b3, ml = lax.optimization_barrier((a3, b3, ml))
    a4, b4 = up(a3[0:2]), down(b3[2:4])
    ml, ot, *keys3 = call(functools.partial(more_kernel, (5, 3)), "third", state + keys, (sc, qt, ml, ot, a3, b3), values)
    ml, o_rows, *keys4 = call(
        last_kernel, "finish", [state[0], ((256, 1024), bf)] + keys, (sc, qt, dt, ml, ot, a4, b4), [part, state[1]] + values
    )
    fixed = (sc, qt, dt, rows, ml)
    dq_state = state[1]
    dq, ga, gb = call(far_kernel, "back4", [dq_state, half, half], fixed + tuple(keys4), acc + [part])
    ga, gb = up(ga), down(gb)
    back = [dq_state, part, part]
    dq, pb, pa = call(functools.partial(pair_kernel, (5, 3)), "back3", back, fixed + (dq, *keys3), acc)
    ga = jnp.concatenate([pa[0:2] + ga, pa[2:4]], axis=0)
    gb = jnp.concatenate([pb[0:2], pb[2:4] + gb], axis=0)
    dq, ga, gb = lax.optimization_barrier((dq, ga, gb))
    ga, gb = up(ga), down(gb)
    dq, pb, pa = call(functools.partial(pair_kernel, (6, 2)), "back2", back, fixed + (dq, *keys2), acc)
    dq, ga, gb = lax.optimization_barrier((dq, pa + ga, pb + gb))
    ga, gb = up(ga), down(gb)
    dq, own = call(own_kernel, "back0", [dq_state, part], fixed + (dq, *keys0, here, nkv, keep), acc)
    dq_rows, pb, pa = call(
        near_grads_kernel, "back1", [((256, 1024), bf), part, part], fixed + (dq, *keys1), [dq_state] + acc
    )
    dq_rows, ga, gb = lax.optimization_barrier((dq_rows, pa + ga, pb + gb))
    ga, gb = up(ga), down(gb)
    outs = collect(jnp.concatenate([o_rows, dq_rows], axis=1), 4)
    total = (own.astype(f32) + ga.astype(f32) + gb.astype(f32)).astype(bf)
    got = exchange(total.reshape(NX * NH, 32, 256), PLANE).reshape(NX, NH, 32, 256)
    got = jnp.sum(got.astype(f32), axis=0)
    got = jnp.transpose(got, (1, 0, 2)).astype(bf)
    return outs + (got[:, :, 0:128].reshape(32, -1), got[:, :, 128:256].reshape(32, -1))


def solution(mesh):
    tokens = P(("ctx", "head"), None)
    return jax.shard_map(
        on_device,
        mesh=mesh,
        in_specs=(tokens,) * 4 + (P("ctx"), P("ctx"), P(None, "head"), P(None, "head"), tokens, tokens),
        out_specs=(tokens,) * 6,
        check_vma=False,
    )
```

```python
import functools
import math

import jax
import jax.numpy as jnp
from jax import lax
from jax.experimental import pallas as pl
from jax.experimental.pallas import tpu as pltpu
from jax.sharding import PartitionSpec as P

bf = jnp.bfloat16
f32 = jnp.float32
BLOCK = 32
LEVELS = 8
NX, NZ, NH = 4, 8, 8
C = 256
W = 1024
NEG = -1e30
SC = 1.0 / math.sqrt(128)
C2 = math.log2(math.e) * SC


def dot(a, b):
    return jnp.dot(a, b, preferred_element_type=f32)


def flip(a):
    return a.astype(f32).T.astype(bf)


def cols(part, stream):
    return slice(part * W + stream * 512, part * W + stream * 512 + 512)


def tiles():
    for part in range(2):
        for t in range(8):
            at = part * W + t * 128
            yield slice(at, at + 128), slice(part * 128, part * 128 + 128), slice(t * 128, t * 128 + 128)


def masks():
    key_block = lax.broadcasted_iota(jnp.int32, (C, 512), 0) // BLOCK
    row_block = (lax.broadcasted_iota(jnp.int32, (C, 512), 1) % 128) // 16
    return key_block, row_block


def chunks(j, n=1):
    return pl.ds(pl.multiple_of(j * C, C), n * C)


def group_bounds(sc_ref, offset):
    z = sc_ref[2]
    earlier = (lax.rem(z + offset, NZ) < z).astype(jnp.int32)
    return sc_ref[0] + earlier, sc_ref[1] + earlier


class Plan:
    def __init__(self, sc_ref, groups):
        self.groups = [kv_ref for _, kv_ref in groups]
        self.bounds = [group_bounds(sc_ref, offset) for offset, _ in groups]
        self.early = sum(low for low, _ in self.bounds)
        self.late = sum(high for _, high in self.bounds)

    def place(self, g, i):
        low, _ = self.bounds[g]
        low_base, high_base = 0, self.early
        if g:
            low_base = self.bounds[0][0]
            high_base = self.early + self.bounds[0][1] - self.bounds[0][0]
        return jnp.where(i < low, low_base + i, high_base + i - low)

    def each(self, body):
        for g, kv_ref in enumerate(self.groups):

            def one(i, _):
                body(self.place(g, i), kv_ref[i])
                return 0

            lax.fori_loop(0, self.bounds[g][1], one, 0)

    def sweep(self, unit):
        room = NX * len(self.groups)
        late, early = self.late // 2, self.early // 2

        def double(k, _):
            part = (k < late).astype(jnp.int32)
            j = jnp.where(part == 1, k, k - late) * 2
            unit(j, 2, pl.ds(pl.multiple_of(part * W, W), W), j + (1 - part) * room)
            return 0

        lax.fori_loop(0, late + early, double, 0)
        late_left, early_left = self.late - 2 * late, self.early - 2 * early

        def single(k, _):
            part = (k < late_left).astype(jnp.int32)
            j = jnp.where(part == 1, 2 * late, 2 * early)
            unit(j, 1, pl.ds(pl.multiple_of(part * W, W), W), j + (1 - part) * room)
            return 0

        lax.fori_loop(0, late_left + early_left, single, 0)


def fold(kv, qt, ml, ot, sl, mask=None):
    s = dot(kv[:, 0:128], qt[:, sl]) * C2
    if mask is not None:
        s = jnp.where(mask, s, NEG)
    old = ml[0:1, sl]
    m = jnp.maximum(old, jnp.max(s, axis=0, keepdims=True))
    p = jnp.exp2(s - m)
    a = jnp.exp2(old - m)
    ml[0:1, sl] = m
    ml[1:2, sl] = ml[1:2, sl] * a + jnp.sum(p, axis=0, keepdims=True)
    ot[:, sl] = ot[:, sl] * a + dot(flip(kv[:, 128:256]), p.astype(bf))


def first(kv, qt, ml, ot, sl, mask):
    s = jnp.where(mask, dot(kv[:, 0:128], qt[:, sl]) * C2, NEG)
    m = jnp.max(s, axis=0, keepdims=True)
    p = jnp.exp2(s - m)
    ml[0:1, sl] = m
    ml[1:2, sl] = jnp.sum(p, axis=0, keepdims=True)
    ot[:, sl] = dot(flip(kv[:, 128:256]), p.astype(bf))


def fold_slow(plan, qt, ml, ot):
    for g, kv_ref in enumerate(plan.groups):
        low, high = plan.bounds[g]

        def one(k, _):
            part = (k < high).astype(jnp.int32)
            fold(kv_ref[k - (1 - part) * high], qt, ml, ot, pl.ds(pl.multiple_of(part * W, W), W))
            return 0

        lax.fori_loop(0, low + high, one, 0)


def fold_groups(sc_ref, groups, qt, ml, ot, ml_old, ot_old, vs, kt, ps, ks, vt):
    ml[...] = ml_old[...]
    ot[...] = ot_old[...]
    plan = Plan(sc_ref, groups)

    def prepare(j, kv):
        ks[chunks(j), :] = kv[:, 0:128]
        vs[chunks(j), :] = kv[:, 128:256]
        kt[:, chunks(j)] = flip(kv[:, 0:128])
        vt[:, chunks(j)] = flip(kv[:, 128:256])

    plan.each(prepare)

    def weigh(j, n, sl, at):
        p = jnp.exp2(dot(ks[chunks(j, n), :], qt[:, sl]) * C2 - ml[0:1, sl])
        rounded = p.astype(bf)
        ps[chunks(at, n), :] = rounded
        return p, rounded

    def unit(j, n, sl, at):
        p, rounded = weigh(j, n, sl, at)
        ml[1:2, sl] = ml[1:2, sl] + jnp.sum(p, axis=0, keepdims=True)
        ot[:, sl] = ot[:, sl] + dot(vt[:, chunks(j, n)], rounded)

    plan.sweep(unit)

    @pl.when(jnp.logical_not(jnp.max(ml[1:2, :]) < 2.0**64))
    def _():
        ml[...] = ml_old[...]
        ot[...] = ot_old[...]
        fold_slow(plan, qt, ml, ot)

        def again(j, n, sl, at):
            weigh(j, n, sl, at)

        plan.sweep(again)

    ml[3:4, :] = ml[0:1, :]


def begin_kernel(sc_ref, qd_ref, kv_ref, nkv_ref, qt, dt, rows, ml_out, ot_out, vs, kt, ps, ks, vt, ml, ot):
    for sl, here, at in tiles():
        q = qd_ref[here, at]
        d = qd_ref[here, 1024 + at.start : 1024 + at.stop]
        rows[sl, 0:128] = q
        rows[sl, 128:256] = d
        qt[:, sl] = flip(q)
        dt[:, sl] = flip(d)
    ml[...] = jnp.zeros_like(ml)
    kb, rb = masks()
    for part in range(2):
        own = kv_ref[sc_ref[part]]
        first(own, qt, ml, ot, cols(part, 0), kb <= rb)
        first(nkv_ref[part], qt, ml, ot, cols(part, 1), kb == rb)
        fold(own, qt, ml, ot, cols(part, 1), kb < rb)
    fold_groups(sc_ref, [(0, kv_ref)], qt, ml_out, ot_out, ml, ot, vs, kt, ps, ks, vt)


def more_kernel(offsets, sc_ref, qt, ml_in, ot_in, ka_ref, kb_ref, ml, ot, vs, kt, ps, ks, vt):
    fold_groups(sc_ref, list(zip(offsets, (ka_ref, kb_ref))), qt, ml, ot, ml_in, ot_in, vs, kt, ps, ks, vt)


def last_kernel(sc_ref, qt, dt, ml_in, ot_in, ka_ref, kb_ref, ml, o_ref, vs, kt, ps, kv, ot, ks, vt):
    kv[0:2] = ka_ref[...]
    kv[2:4] = kb_ref[...]
    fold_groups(sc_ref, [(4, kv)], qt, ml, ot, ml_in, ot_in, vs, kt, ps, ks, vt)
    total = ml[1:2, :]
    inverse = 1.0 / total
    ml[0:1, :] = ml[0:1, :] + jnp.log2(total)
    for sl, here, at in tiles():
        o = ot[:, sl] * inverse[:, sl]
        ml[2:3, sl] = jnp.sum(o * dt[:, sl].astype(f32), axis=0, keepdims=True)
        o_ref[here, at] = o.T.astype(bf)


def grads(k, v, kt, qt, dt, rows, ml, dq, sl, mask=None):
    s = dot(k, qt[:, sl]) * C2
    if mask is not None:
        s = jnp.where(mask, s, NEG)
    p = jnp.exp2(s - ml[0:1, sl])
    ds = (p * (dot(v, dt[:, sl]) - ml[2:3, sl])).astype(bf)
    dq[:, sl] = dq[:, sl] + dot(kt, ds)
    return dot(ds, rows[sl, 0:128]), dot(p.astype(bf), rows[sl, 128:256])


def grad_groups(sc_ref, offsets, dt, rows, ml, dq, mk, vs, kt, ps, acc):
    plan = Plan(sc_ref, [(offset, None) for offset in offsets])

    def clear(j, _):
        acc[chunks(j), :] = jnp.zeros((C, 256), f32)
        return 0

    lax.fori_loop(0, plan.late, clear, 0)

    def unit(j, n, sl, at):
        keys = chunks(j, n)
        p = ps[chunks(at, n), :].astype(f32) * jnp.exp2(mk[3:4, sl] - ml[0:1, sl])
        ds = (p * (dot(vs[keys, :], dt[:, sl]) - ml[2:3, sl])).astype(bf)
        dq[:, sl] = dq[:, sl] + dot(kt[:, keys], ds)
        acc[keys, 0:128] += dot(ds, rows[sl, 0:128])
        acc[keys, 128:256] += dot(p.astype(bf), rows[sl, 128:256])

    plan.sweep(unit)
    return plan


def hand_over(plan, acc, outs):
    for g, put in enumerate(outs):
        high = plan.bounds[g][1]

        def some(i, _):
            j = chunks(plan.place(g, i))
            put(i, jnp.concatenate([acc[j, 0:128] * SC, acc[j, 128:256]], axis=1).astype(bf))
            return 0

        def none(i, _):
            put(i, jnp.zeros((C, 256), bf))
            return 0

        lax.fori_loop(0, high, some, 0)
        lax.fori_loop(high, NX, none, 0)


def into(ref):
    def put(i, value):
        ref[i] = value

    return put


def far_kernel(sc_ref, dt, rows, ml, mk, vs, kt, ps, dq, oa, ob, acc, out):
    dq[...] = jnp.zeros_like(dq)
    plan = grad_groups(sc_ref, (4,), dt, rows, ml, dq, mk, vs, kt, ps, acc)
    hand_over(plan, acc, [into(out)])
    oa[...] = out[0:2]
    ob[...] = out[2:4]


def pair_kernel(offsets, sc_ref, dt, rows, ml, dq_in, mk, vs, kt, ps, dq, oa, ob, acc):
    dq[...] = dq_in[...]
    plan = grad_groups(sc_ref, offsets, dt, rows, ml, dq, mk, vs, kt, ps, acc)
    hand_over(plan, acc, [into(oa), into(ob)])


def own_kernel(sc_ref, dt, rows, ml, dq_in, mk, vs, kt, ps, qt, kv_ref, nkv_ref, keep_ref, dq, out, acc):
    dq[...] = dq_in[...]
    plan = grad_groups(sc_ref, (0,), dt, rows, ml, dq, mk, vs, kt, ps, acc)
    kb, rb = masks()
    for part in range(2):
        i = sc_ref[part]
        own, noised = kv_ref[i], nkv_ref[part]
        k, v, turned = own[:, 0:128], own[:, 128:256], flip(own[:, 0:128])
        ka, va = grads(k, v, turned, qt, dt, rows, ml, dq, cols(part, 0), kb <= rb)
        kc, vc = grads(k, v, turned, qt, dt, rows, ml, dq, cols(part, 1), kb < rb)
        k, v, turned = noised[:, 0:128], noised[:, 128:256], flip(noised[:, 0:128])
        kn, vn = grads(k, v, turned, qt, dt, rows, ml, dq, cols(part, 1), kb == rb)
        keep = keep_ref[part]
        seen = i < plan.late
        before = acc[chunks(i), :]
        acc[chunks(i), 0:128] = jnp.where(seen, before[:, 0:128], 0.0) + ka + kc + kn * keep
        acc[chunks(i), 128:256] = jnp.where(seen, before[:, 128:256], 0.0) + va + vc + vn * keep
    plan.bounds = [(plan.bounds[0][0], plan.bounds[0][1] + 1)]

    hand_over(plan, acc, [into(out)])


def near_grads_kernel(sc_ref, dt, rows, ml, dq_in, mk, vs, kt, ps, o_rows, q_rows, oa, ob, dq, acc):
    pair_kernel((7, 1), sc_ref, dt, rows, ml, dq_in, mk, vs, kt, ps, dq, oa, ob, acc)
    q_rows[:, 0:1024] = o_rows[...]
    for sl, here, at in tiles():
        q_rows[here, 1024 + at.start : 1024 + at.stop] = (dq[:, sl] * SC).T.astype(bf)


def unpack_kv_kernel(sc_ref, got, dk, dv):
    for h in range(NH):
        total = got[h].astype(f32)
        for x in range(1, NX):
            total = total + got[x * NH + h].astype(f32)
        dk[:, h * 128 : h * 128 + 128] = total[:, 0:128].astype(bf)
        dv[:, h * 128 : h * 128 + 128] = total[:, 128:256].astype(bf)


def call(body, name, outs, args, scratch):
    vm = pl.BlockSpec(memory_space=pltpu.VMEM)
    return pl.pallas_call(
        body,
        out_shape=tuple(jax.ShapeDtypeStruct(*o) for o in outs),
        in_specs=[pl.BlockSpec(memory_space=pltpu.SMEM)] + [vm] * (len(args) - 1),
        out_specs=(vm,) * len(outs),
        scratch_shapes=[pltpu.VMEM(*s) for s in scratch],
        compiler_params=pltpu.CompilerParams(vmem_limit_bytes=20 * 1024 * 1024),
        cost_estimate=pl.CostEstimate(flops=200_000_000, bytes_accessed=1_000_000, transcendentals=1_000_000),
        name=name,
    )(*args)


def device(x, z, h):
    return (x * NZ + z) * NH + h


BOTH = ("ctx", "head")
PLANE = [[device(x, z, h) for x in range(NX) for h in range(NH)] for z in range(NZ)]
MIRROR = [[device(x, z, h) for x in (a, NX - 1 - a) for h in range(NH)] for z in range(NZ) for a in range(2)]
UP = [(x * NZ + z, x * NZ + (z + 1) % NZ) for x in range(NX) for z in range(NZ)]
DOWN = [(x * NZ + z, x * NZ + (z - 1) % NZ) for x in range(NX) for z in range(NZ)]
SWAP = [(x * NZ + z, (NX - 1 - x) * NZ + z) for x in range(NX) for z in range(NZ)]


def exchange(a, groups):
    return lax.all_to_all(a, BOTH, split_axis=0, concat_axis=0, tiled=True, axis_index_groups=groups)


def up(a):
    return lax.ppermute(a, "ctx", UP)


def down(a):
    return lax.ppermute(a, "ctx", DOWN)


def spread(parts):
    cut = [jnp.transpose(p.reshape(2, 16, NH, 512), (0, 2, 1, 3)) for p in parts]
    sent = jnp.concatenate(cut, axis=3).reshape(16, 16, -1)
    return exchange(sent, MIRROR).reshape(256, -1)


def collect(rows, parts):
    got = exchange(rows.reshape(16, 16, -1), MIRROR).reshape(2, NH, 16, parts, 512)
    return tuple(jnp.transpose(got[:, :, :, i], (0, 2, 1, 3)).reshape(32, -1) for i in range(parts))


def on_device(q_clean, k_clean, v_clean, q_noised, masked, noise_level, mask_key, mask_value, d_clean, d_noised):
    ctx = lax.axis_index("ctx")
    x, z = ctx // NZ, ctx % NZ
    lo = jnp.minimum(x, NX - 1 - x)
    sc = jnp.stack([lo, NX - 1 - lo, z]).astype(jnp.int32)

    kv = jnp.concatenate([k_clean.reshape(32, NH, 128), v_clean.reshape(32, NH, 128)], axis=2)
    kv = jnp.broadcast_to(jnp.transpose(kv, (1, 0, 2))[None], (NX, NH, 32, 256)).reshape(NX * NH, 32, 256)
    here = exchange(kv, PLANE).reshape(NX, C, 256)
    qd = spread((q_clean, q_noised, d_clean, d_noised))
    info = jnp.concatenate([masked, noise_level])
    other = lax.ppermute(info, "ctx", SWAP)
    info = jnp.where(x < 2, jnp.stack([info, other]), jnp.stack([other, info]))
    covered = info[:, :C] == 1
    onehot = (info[:, C:, None] == jnp.arange(LEVELS, dtype=jnp.int32)).astype(bf)
    table = dot(onehot.reshape(16, LEVELS), jnp.concatenate([mask_key, mask_value], axis=1)).astype(bf)
    table = jnp.repeat(table, BLOCK, axis=0).reshape(2, C, 256)
    mine = jnp.stack([lax.dynamic_index_in_dim(here, sc[i], 0, keepdims=False) for i in range(2)])
    nkv = jnp.where(covered[:, :, None], table, mine)
    keep = jnp.broadcast_to((info[:, :C] == 0).astype(f32)[:, :, None], (2, C, 128))

    a1, b1 = up(here), down(here)
    a2, b2 = up(a1), down(b1)
    state = [((8, 2 * W), f32), ((128, 2 * W), f32)]
    turned = ((128, 2 * W), bf)
    part = ((NX, C, 256), bf)
    half = ((2, C, 256), bf)
    keys = [((8 * C, 128), bf), ((128, 8 * C), bf)]
    one, two = keys + [((6 * C, W), bf)], keys + [((12 * C, W), bf)]
    acc = [((8 * C, 256), f32)]
    qt, dt, rows, ml0, ot, *keys0 = call(
        begin_kernel, "begin", [turned, turned, ((2 * W, 256), bf)] + state + one, (sc, qd, here, nkv), keys + state
    )
    a2, b2, ml0 = lax.optimization_barrier((a2, b2, ml0))
    a3, b3 = up(a2), down(b2)
    ml1, ot, *keys1 = call(functools.partial(more_kernel, (7, 1)), "near", state + two, (sc, qt, ml0, ot, a1, b1), keys)
    ml2, ot, *keys2 = call(functools.partial(more_kernel, (6, 2)), "second", state + two, (sc, qt, ml1, ot, a2, b2), keys)
    a3, b3, ml2 = lax.optimization_barrier((a3, b3, ml2))
    a4, b4 = up(a3[0:2]), down(b3[2:4])
    ml3, ot, *keys3 = call(functools.partial(more_kernel, (5, 3)), "third", state + two, (sc, qt, ml2, ot, a3, b3), keys)
    ml, o_rows, *keys4 = call(
        last_kernel, "finish", [state[0], ((256, 1024), bf)] + one, (sc, qt, dt, ml3, ot, a4, b4), [part, state[1]] + keys
    )
    fixed = (sc, dt, rows, ml)
    dq_state = state[1]
    dq, ga, gb = call(far_kernel, "back4", [dq_state, half, half], fixed + (ml, *keys4), acc + [part])
    ga, gb = up(ga), down(gb)
    back = [dq_state, part, part]
    dq, pb, pa = call(functools.partial(pair_kernel, (5, 3)), "back3", back, fixed + (dq, ml3, *keys3), acc)
    ga = jnp.concatenate([pa[0:2] + ga, pa[2:4]], axis=0)
    gb = jnp.concatenate([pb[0:2], pb[2:4] + gb], axis=0)
    dq, ga, gb = lax.optimization_barrier((dq, ga, gb))
    ga, gb = up(ga), down(gb)
    dq, pb, pa = call(functools.partial(pair_kernel, (6, 2)), "back2", back, fixed + (dq, ml2, *keys2), acc)
    dq, ga, gb = lax.optimization_barrier((dq, pa + ga, pb + gb))
    ga, gb = up(ga), down(gb)
    dq, own = call(own_kernel, "back0", [dq_state, part], fixed + (dq, ml0, *keys0, qt, here, nkv, keep), acc)
    q_rows, pb, pa = call(
        near_grads_kernel, "back1", [((256, 2048), bf), part, part], fixed + (dq, ml1, *keys1, o_rows), [dq_state] + acc
    )
    q_rows, ga, gb = lax.optimization_barrier((q_rows, pa + ga, pb + gb))
    ga, gb = up(ga), down(gb)
    outs = collect(q_rows, 4)
    total = (own.astype(f32) + ga.astype(f32) + gb.astype(f32)).astype(bf)
    got = exchange(total.reshape(NX * NH, 32, 256), PLANE)
    return outs + tuple(call(unpack_kv_kernel, "unpack_kv", [((32, 1024), bf)] * 2, (sc, got), []))


def solution(mesh):
    tokens = P(("ctx", "head"), None)
    return jax.shard_map(
        on_device,
        mesh=mesh,
        in_specs=(tokens,) * 4 + (P("ctx"), P("ctx"), P(None, "head"), P(None, "head"), tokens, tokens),
        out_specs=(tokens,) * 6,
        check_vma=False,
    )
```

```python
import functools
import math

import jax
import jax.numpy as jnp
from jax import lax
from jax.experimental import pallas as pl
from jax.experimental.pallas import tpu as pltpu
from jax.sharding import PartitionSpec as P

bf = jnp.bfloat16
f32 = jnp.float32
BLOCK = 32
LEVELS = 8
NX, NZ, NH = 4, 8, 8
C = 256
W = 1024
NEG = -1e30
SC = 1.0 / math.sqrt(128)
C2 = math.log2(math.e) * SC


def dot(a, b):
    return jnp.dot(a, b, preferred_element_type=f32)


def flip(a):
    return a.astype(f32).T.astype(bf)


def cols(part, stream):
    return slice(part * W + stream * 512, part * W + stream * 512 + 512)


def tiles():
    for part in range(2):
        for t in range(8):
            at = part * W + t * 128
            yield slice(at, at + 128), slice(part * 128, part * 128 + 128), slice(t * 128, t * 128 + 128)


def masks():
    key_block = lax.broadcasted_iota(jnp.int32, (C, 512), 0) // BLOCK
    row_block = (lax.broadcasted_iota(jnp.int32, (C, 512), 1) % 128) // 16
    return key_block, row_block


def chunks(j, n=1):
    return pl.ds(pl.multiple_of(j * C, C), n * C)


def group_bounds(sc_ref, offset):
    z = sc_ref[2]
    earlier = (lax.rem(z + offset, NZ) < z).astype(jnp.int32)
    return sc_ref[0] + earlier, sc_ref[1] + earlier


class Plan:
    def __init__(self, sc_ref, groups):
        self.groups = [kv_ref for _, kv_ref in groups]
        self.bounds = [group_bounds(sc_ref, offset) for offset, _ in groups]
        self.early = sum(low for low, _ in self.bounds)
        self.late = sum(high for _, high in self.bounds)

    def place(self, g, i):
        low, _ = self.bounds[g]
        low_base, high_base = 0, self.early
        if g:
            low_base = self.bounds[0][0]
            high_base = self.early + self.bounds[0][1] - self.bounds[0][0]
        return jnp.where(i < low, low_base + i, high_base + i - low)

    def each(self, body):
        for g, kv_ref in enumerate(self.groups):

            def one(i, _):
                body(self.place(g, i), kv_ref[i])
                return 0

            lax.fori_loop(0, self.bounds[g][1], one, 0)

    def sweep(self, unit):
        room = NX * len(self.groups)
        late, early = self.late // 2, self.early // 2

        def double(k, _):
            part = (k < late).astype(jnp.int32)
            j = jnp.where(part == 1, k, k - late) * 2
            unit(j, 2, pl.ds(pl.multiple_of(part * W, W), W), j + (1 - part) * room)
            return 0

        lax.fori_loop(0, late + early, double, 0)
        late_left, early_left = self.late - 2 * late, self.early - 2 * early

        def single(k, _):
            part = (k < late_left).astype(jnp.int32)
            j = jnp.where(part == 1, 2 * late, 2 * early)
            unit(j, 1, pl.ds(pl.multiple_of(part * W, W), W), j + (1 - part) * room)
            return 0

        lax.fori_loop(0, late_left + early_left, single, 0)


    def crawl(self, unit):
        room = NX * len(self.groups)

        def one(k, _):
            half = lax.rem(k, 2)
            k = k // 2
            part = (k < self.late).astype(jnp.int32)
            j = k - (1 - part) * self.late
            unit(j, pl.ds(pl.multiple_of(part * W + half * 512, 512), 512), j + (1 - part) * room, half)
            return 0

        lax.fori_loop(0, 2 * (self.late + self.early), one, 0)


def fold(k, vt, qt, ml, ot, sl, mask=None):
    s = dot(k, qt[:, sl]) * C2
    if mask is not None:
        s = jnp.where(mask, s, NEG)
    old = ml[0:1, sl]
    m = jnp.maximum(old, jnp.max(s, axis=0, keepdims=True))
    p = jnp.exp2(s - m)
    a = jnp.exp2(old - m)
    ml[0:1, sl] = m
    ml[1:2, sl] = ml[1:2, sl] * a + jnp.sum(p, axis=0, keepdims=True)
    ot[:, sl] = ot[:, sl] * a + dot(vt, p.astype(bf))


def first(kv, qt, ml, ot, sl, mask):
    s = jnp.where(mask, dot(kv[:, 0:128], qt[:, sl]) * C2, NEG)
    m = jnp.max(s, axis=0, keepdims=True)
    p = jnp.exp2(s - m)
    ml[0:1, sl] = m
    ml[1:2, sl] = jnp.sum(p, axis=0, keepdims=True)
    ot[:, sl] = dot(flip(kv[:, 128:256]), p.astype(bf))


def fold_groups(sc_ref, groups, qt, ml, ot, ml_old, ot_old, vs, kt, ps, ks, vt):
    ml[...] = ml_old[...]
    ot[...] = ot_old[...]
    plan = Plan(sc_ref, groups)

    def prepare(j, kv):
        ks[chunks(j), :] = kv[:, 0:128]
        vs[chunks(j), :] = kv[:, 128:256]
        kt[:, chunks(j)] = flip(kv[:, 0:128])
        vt[:, chunks(j)] = flip(kv[:, 128:256])

    plan.each(prepare)

    def unit(j, n, sl, at):
        p = jnp.exp2(dot(ks[chunks(j, n), :], qt[:, sl]) * C2 - ml[0:1, sl])
        rounded = p.astype(bf)
        ps[chunks(at, n), :] = rounded
        ml[1:2, sl] = ml[1:2, sl] + jnp.sum(p, axis=0, keepdims=True)
        ot[:, sl] = ot[:, sl] + dot(vt[:, chunks(j, n)], rounded)

    plan.sweep(unit)

    @pl.when(jnp.logical_not(jnp.max(ml[1:2, :]) < 2.0**64))
    def _():
        ml[...] = ml_old[...]
        ot[...] = ot_old[...]

        def slow(j, sl, at, half):
            fold(ks[chunks(j), :], vt[:, chunks(j)], qt, ml, ot, sl)

        def again(j, sl, at, half):
            p = jnp.exp2(dot(ks[chunks(j), :], qt[:, sl]) * C2 - ml[0:1, sl])
            ps[chunks(at), pl.ds(pl.multiple_of(half * 512, 512), 512)] = p.astype(bf)

        plan.crawl(slow)
        plan.crawl(again)

    ml[3:4, :] = ml[0:1, :]


def begin_kernel(sc_ref, qd_ref, kv_ref, nkv_ref, qt, dt, rows, ml_out, ot_out, vs, kt, ps, ks, vt, ml, ot):
    for sl, here, at in tiles():
        q = qd_ref[here, at]
        d = qd_ref[here, 1024 + at.start : 1024 + at.stop]
        rows[sl, 0:128] = q
        rows[sl, 128:256] = d
        qt[:, sl] = flip(q)
        dt[:, sl] = flip(d)
    ml[...] = jnp.zeros_like(ml)
    kb, rb = masks()
    for part in range(2):
        own = kv_ref[sc_ref[part]]
        first(own, qt, ml, ot, cols(part, 0), kb <= rb)
        first(nkv_ref[part], qt, ml, ot, cols(part, 1), kb == rb)
        fold(own[:, 0:128], flip(own[:, 128:256]), qt, ml, ot, cols(part, 1), kb < rb)
    fold_groups(sc_ref, [(0, kv_ref)], qt, ml_out, ot_out, ml, ot, vs, kt, ps, ks, vt)


def more_kernel(offsets, sc_ref, qt, ml_in, ot_in, ka_ref, kb_ref, ml, ot, vs, kt, ps, ks, vt):
    fold_groups(sc_ref, list(zip(offsets, (ka_ref, kb_ref))), qt, ml, ot, ml_in, ot_in, vs, kt, ps, ks, vt)


def last_kernel(sc_ref, qt, dt, ml_in, ot_in, ka_ref, kb_ref, ml, o_ref, vs, kt, ps, kv, ot, ks, vt):
    kv[0:2] = ka_ref[...]
    kv[2:4] = kb_ref[...]
    fold_groups(sc_ref, [(4, kv)], qt, ml, ot, ml_in, ot_in, vs, kt, ps, ks, vt)
    total = ml[1:2, :]
    inverse = 1.0 / total
    ml[0:1, :] = ml[0:1, :] + jnp.log2(total)
    for sl, here, at in tiles():
        o = ot[:, sl] * inverse[:, sl]
        ml[2:3, sl] = jnp.sum(o * dt[:, sl].astype(f32), axis=0, keepdims=True)
        o_ref[here, at] = o.T.astype(bf)


def grads(k, v, kt, qt, dt, rows, ml, dq, sl, mask=None):
    s = dot(k, qt[:, sl]) * C2
    if mask is not None:
        s = jnp.where(mask, s, NEG)
    p = jnp.exp2(s - ml[0:1, sl])
    ds = (p * (dot(v, dt[:, sl]) - ml[2:3, sl])).astype(bf)
    dq[:, sl] = dq[:, sl] + dot(kt, ds)
    return dot(ds, rows[sl, 0:128]), dot(p.astype(bf), rows[sl, 128:256])


def grad_groups(sc_ref, offsets, dt, rows, ml, dq, mk, vs, kt, ps, acc):
    plan = Plan(sc_ref, [(offset, None) for offset in offsets])

    def clear(j, _):
        acc[chunks(j), :] = jnp.zeros((C, 256), f32)
        return 0

    lax.fori_loop(0, plan.late, clear, 0)

    def unit(j, n, sl, at):
        keys = chunks(j, n)
        p = ps[chunks(at, n), :].astype(f32) * jnp.exp2(mk[3:4, sl] - ml[0:1, sl])
        ds = (p * (dot(vs[keys, :], dt[:, sl]) - ml[2:3, sl])).astype(bf)
        dq[:, sl] = dq[:, sl] + dot(kt[:, keys], ds)
        acc[keys, 0:128] += dot(ds, rows[sl, 0:128])
        acc[keys, 128:256] += dot(p.astype(bf), rows[sl, 128:256])

    plan.sweep(unit)
    return plan


def hand_over(plan, acc, outs):
    for g, put in enumerate(outs):
        high = plan.bounds[g][1]

        def some(i, _):
            j = chunks(plan.place(g, i))
            put(i, jnp.concatenate([acc[j, 0:128] * SC, acc[j, 128:256]], axis=1).astype(bf))
            return 0

        def none(i, _):
            put(i, jnp.zeros((C, 256), bf))
            return 0

        lax.fori_loop(0, high, some, 0)
        lax.fori_loop(high, NX, none, 0)


def into(ref):
    def put(i, value):
        ref[i] = value

    return put


def far_kernel(sc_ref, dt, rows, ml, mk, vs, kt, ps, dq, oa, ob, acc, out):
    dq[...] = jnp.zeros_like(dq)
    plan = grad_groups(sc_ref, (4,), dt, rows, ml, dq, mk, vs, kt, ps, acc)
    hand_over(plan, acc, [into(out)])
    oa[...] = out[0:2]
    ob[...] = out[2:4]


def pair_kernel(offsets, sc_ref, dt, rows, ml, dq_in, mk, vs, kt, ps, dq, oa, ob, acc):
    dq[...] = dq_in[...]
    plan = grad_groups(sc_ref, offsets, dt, rows, ml, dq, mk, vs, kt, ps, acc)
    hand_over(plan, acc, [into(oa), into(ob)])


def own_kernel(sc_ref, dt, rows, ml, dq_in, mk, vs, kt, ps, qt, kv_ref, nkv_ref, keep_ref, dq, out, acc):
    dq[...] = dq_in[...]
    plan = grad_groups(sc_ref, (0,), dt, rows, ml, dq, mk, vs, kt, ps, acc)
    kb, rb = masks()
    for part in range(2):
        i = sc_ref[part]
        own, noised = kv_ref[i], nkv_ref[part]
        k, v, turned = own[:, 0:128], own[:, 128:256], flip(own[:, 0:128])
        ka, va = grads(k, v, turned, qt, dt, rows, ml, dq, cols(part, 0), kb <= rb)
        kc, vc = grads(k, v, turned, qt, dt, rows, ml, dq, cols(part, 1), kb < rb)
        k, v, turned = noised[:, 0:128], noised[:, 128:256], flip(noised[:, 0:128])
        kn, vn = grads(k, v, turned, qt, dt, rows, ml, dq, cols(part, 1), kb == rb)
        keep = keep_ref[part]
        seen = i < plan.late
        before = acc[chunks(i), :]
        acc[chunks(i), 0:128] = jnp.where(seen, before[:, 0:128], 0.0) + ka + kc + kn * keep
        acc[chunks(i), 128:256] = jnp.where(seen, before[:, 128:256], 0.0) + va + vc + vn * keep
    plan.bounds = [(plan.bounds[0][0], plan.bounds[0][1] + 1)]

    hand_over(plan, acc, [into(out)])


def near_grads_kernel(sc_ref, dt, rows, ml, dq_in, mk, vs, kt, ps, o_rows, q_rows, oa, ob, dq, acc):
    pair_kernel((7, 1), sc_ref, dt, rows, ml, dq_in, mk, vs, kt, ps, dq, oa, ob, acc)
    q_rows[:, 0:1024] = o_rows[...]
    for sl, here, at in tiles():
        q_rows[here, 1024 + at.start : 1024 + at.stop] = (dq[:, sl] * SC).T.astype(bf)


def unpack_kv_kernel(sc_ref, got, dk, dv):
    for h in range(NH):
        total = got[h].astype(f32)
        for x in range(1, NX):
            total = total + got[x * NH + h].astype(f32)
        dk[:, h * 128 : h * 128 + 128] = total[:, 0:128].astype(bf)
        dv[:, h * 128 : h * 128 + 128] = total[:, 128:256].astype(bf)


def call(body, name, outs, args, scratch):
    vm = pl.BlockSpec(memory_space=pltpu.VMEM)
    return pl.pallas_call(
        body,
        out_shape=tuple(jax.ShapeDtypeStruct(*o) for o in outs),
        in_specs=[pl.BlockSpec(memory_space=pltpu.SMEM)] + [vm] * (len(args) - 1),
        out_specs=(vm,) * len(outs),
        scratch_shapes=[pltpu.VMEM(*s) for s in scratch],
        compiler_params=pltpu.CompilerParams(vmem_limit_bytes=20 * 1024 * 1024),
        cost_estimate=pl.CostEstimate(flops=200_000_000, bytes_accessed=1_000_000, transcendentals=1_000_000),
        name=name,
    )(*args)


def device(x, z, h):
    return (x * NZ + z) * NH + h


BOTH = ("ctx", "head")
PLANE = [[device(x, z, h) for x in range(NX) for h in range(NH)] for z in range(NZ)]
MIRROR = [[device(x, z, h) for x in (a, NX - 1 - a) for h in range(NH)] for z in range(NZ) for a in range(2)]
UP = [(x * NZ + z, x * NZ + (z + 1) % NZ) for x in range(NX) for z in range(NZ)]
DOWN = [(x * NZ + z, x * NZ + (z - 1) % NZ) for x in range(NX) for z in range(NZ)]
SWAP = [(x * NZ + z, (NX - 1 - x) * NZ + z) for x in range(NX) for z in range(NZ)]


def exchange(a, groups):
    return lax.all_to_all(a, BOTH, split_axis=0, concat_axis=0, tiled=True, axis_index_groups=groups)


def up(a):
    return lax.ppermute(a, "ctx", UP)


def down(a):
    return lax.ppermute(a, "ctx", DOWN)


def spread(parts):
    cut = [jnp.transpose(p.reshape(2, 16, NH, 512), (0, 2, 1, 3)) for p in parts]
    sent = jnp.concatenate(cut, axis=3).reshape(16, 16, -1)
    return exchange(sent, MIRROR).reshape(256, -1)


def collect(rows, parts):
    got = exchange(rows.reshape(16, 16, -1), MIRROR).reshape(2, NH, 16, parts, 512)
    return tuple(jnp.transpose(got[:, :, :, i], (0, 2, 1, 3)).reshape(32, -1) for i in range(parts))


def on_device(q_clean, k_clean, v_clean, q_noised, masked, noise_level, mask_key, mask_value, d_clean, d_noised):
    ctx = lax.axis_index("ctx")
    x, z = ctx // NZ, ctx % NZ
    lo = jnp.minimum(x, NX - 1 - x)
    sc = jnp.stack([lo, NX - 1 - lo, z]).astype(jnp.int32)

    kv = jnp.concatenate([k_clean.reshape(32, NH, 128), v_clean.reshape(32, NH, 128)], axis=2)
    kv = jnp.broadcast_to(jnp.transpose(kv, (1, 0, 2))[None], (NX, NH, 32, 256)).reshape(NX * NH, 32, 256)
    here = exchange(kv, PLANE).reshape(NX, C, 256)
    qd = spread((q_clean, q_noised, d_clean, d_noised))
    info = jnp.concatenate([masked, noise_level])
    other = lax.ppermute(info, "ctx", SWAP)
    info = jnp.where(x < 2, jnp.stack([info, other]), jnp.stack([other, info]))
    covered = info[:, :C] == 1
    onehot = (info[:, C:, None] == jnp.arange(LEVELS, dtype=jnp.int32)).astype(bf)
    table = dot(onehot.reshape(16, LEVELS), jnp.concatenate([mask_key, mask_value], axis=1)).astype(bf)
    table = jnp.repeat(table, BLOCK, axis=0).reshape(2, C, 256)
    mine = jnp.stack([lax.dynamic_index_in_dim(here, sc[i], 0, keepdims=False) for i in range(2)])
    nkv = jnp.where(covered[:, :, None], table, mine)
    keep = jnp.broadcast_to((info[:, :C] == 0).astype(f32)[:, :, None], (2, C, 128))

    a1, b1 = up(here), down(here)
    a2, b2 = up(a1), down(b1)
    state = [((8, 2 * W), f32), ((128, 2 * W), f32)]
    turned = ((128, 2 * W), bf)
    part = ((NX, C, 256), bf)
    half = ((2, C, 256), bf)
    keys = [((8 * C, 128), bf), ((128, 8 * C), bf)]
    one, two = keys + [((6 * C, W), bf)], keys + [((12 * C, W), bf)]
    acc = [((8 * C, 256), f32)]
    qt, dt, rows, ml0, ot, *keys0 = call(
        begin_kernel, "begin", [turned, turned, ((2 * W, 256), bf)] + state + one, (sc, qd, here, nkv), keys + state
    )
    a2, b2, ml0 = lax.optimization_barrier((a2, b2, ml0))
    a3, b3 = up(a2), down(b2)
    ml1, ot, *keys1 = call(functools.partial(more_kernel, (7, 1)), "near", state + two, (sc, qt, ml0, ot, a1, b1), keys)
    ml2, ot, *keys2 = call(functools.partial(more_kernel, (6, 2)), "second", state + two, (sc, qt, ml1, ot, a2, b2), keys)
    a3, b3, ml2 = lax.optimization_barrier((a3, b3, ml2))
    a4, b4 = up(a3[0:2]), down(b3[2:4])
    ml3, ot, *keys3 = call(functools.partial(more_kernel, (5, 3)), "third", state + two, (sc, qt, ml2, ot, a3, b3), keys)
    ml, o_rows, *keys4 = call(
        last_kernel, "finish", [state[0], ((256, 1024), bf)] + one, (sc, qt, dt, ml3, ot, a4, b4), [part, state[1]] + keys
    )
    fixed = (sc, dt, rows, ml)
    dq_state = state[1]
    dq, ga, gb = call(far_kernel, "back4", [dq_state, half, half], fixed + (ml, *keys4), acc + [part])
    ga, gb = up(ga), down(gb)
    back = [dq_state, part, part]
    dq, pb, pa = call(functools.partial(pair_kernel, (5, 3)), "back3", back, fixed + (dq, ml3, *keys3), acc)
    ga = jnp.concatenate([pa[0:2] + ga, pa[2:4]], axis=0)
    gb = jnp.concatenate([pb[0:2], pb[2:4] + gb], axis=0)
    dq, ga, gb = lax.optimization_barrier((dq, ga, gb))
    ga, gb = up(ga), down(gb)
    dq, pb, pa = call(functools.partial(pair_kernel, (6, 2)), "back2", back, fixed + (dq, ml2, *keys2), acc)
    dq, ga, gb = lax.optimization_barrier((dq, pa + ga, pb + gb))
    ga, gb = up(ga), down(gb)
    dq, own = call(own_kernel, "back0", [dq_state, part], fixed + (dq, ml0, *keys0, qt, here, nkv, keep), acc)
    q_rows, pb, pa = call(
        near_grads_kernel, "back1", [((256, 2048), bf), part, part], fixed + (dq, ml1, *keys1, o_rows), [dq_state] + acc
    )
    q_rows, ga, gb = lax.optimization_barrier((q_rows, pa + ga, pb + gb))
    ga, gb = up(ga), down(gb)
    outs = collect(q_rows, 4)
    total = (own.astype(f32) + ga.astype(f32) + gb.astype(f32)).astype(bf)
    got = exchange(total.reshape(NX * NH, 32, 256), PLANE)
    return outs + tuple(call(unpack_kv_kernel, "unpack_kv", [((32, 1024), bf)] * 2, (sc, got), []))


def solution(mesh):
    tokens = P(("ctx", "head"), None)
    return jax.shard_map(
        on_device,
        mesh=mesh,
        in_specs=(tokens,) * 4 + (P("ctx"), P("ctx"), P(None, "head"), P(None, "head"), tokens, tokens),
        out_specs=(tokens,) * 6,
        check_vma=False,
    )
```

```python
import functools
import math

import jax
import jax.numpy as jnp
from jax import lax
from jax.experimental import pallas as pl
from jax.experimental.pallas import tpu as pltpu
from jax.sharding import PartitionSpec as P

bf = jnp.bfloat16
f32 = jnp.float32
BLOCK = 32
LEVELS = 8
NX, NZ, NH = 4, 8, 8
C = 256
W = 1024
NEG = -1e30
SC = 1.0 / math.sqrt(128)
C2 = math.log2(math.e) * SC


def dot(a, b):
    return jnp.dot(a, b, preferred_element_type=f32)


def flip(a):
    return a.astype(f32).T.astype(bf)


def cols(part, stream):
    return slice(part * W + stream * 512, part * W + stream * 512 + 512)


def tiles():
    for part in range(2):
        for t in range(8):
            at = part * W + t * 128
            yield slice(at, at + 128), slice(part * 128, part * 128 + 128), slice(t * 128, t * 128 + 128)


def masks():
    key_block = lax.broadcasted_iota(jnp.int32, (C, 512), 0) // BLOCK
    row_block = (lax.broadcasted_iota(jnp.int32, (C, 512), 1) % 128) // 16
    return key_block, row_block


def chunks(j, n=1):
    return pl.ds(pl.multiple_of(j * C, C), n * C)


def group_bounds(sc_ref, offset):
    z = sc_ref[2]
    earlier = (lax.rem(z + offset, NZ) < z).astype(jnp.int32)
    return sc_ref[0] + earlier, sc_ref[1] + earlier


class Plan:
    def __init__(self, sc_ref, groups):
        self.groups = [kv_ref for _, kv_ref in groups]
        self.bounds = [group_bounds(sc_ref, offset) for offset, _ in groups]
        self.early = sum(low for low, _ in self.bounds)
        self.late = sum(high for _, high in self.bounds)

    def place(self, g, i):
        low, _ = self.bounds[g]
        low_base, high_base = 0, self.early
        if g:
            low_base = self.bounds[0][0]
            high_base = self.early + self.bounds[0][1] - self.bounds[0][0]
        return jnp.where(i < low, low_base + i, high_base + i - low)

    def each(self, body):
        for g, kv_ref in enumerate(self.groups):

            def one(i, _):
                body(self.place(g, i), kv_ref[i])
                return 0

            lax.fori_loop(0, self.bounds[g][1], one, 0)

    def sweep(self, unit):
        room = NX * len(self.groups)
        late, early = self.late // 2, self.early // 2

        def double(k, _):
            part = (k < late).astype(jnp.int32)
            j = jnp.where(part == 1, k, k - late) * 2
            unit(j, 2, pl.ds(pl.multiple_of(part * W, W), W), j + (1 - part) * room)
            return 0

        lax.fori_loop(0, late + early, double, 0)
        late_left, early_left = self.late - 2 * late, self.early - 2 * early

        def single(k, _):
            part = (k < late_left).astype(jnp.int32)
            j = jnp.where(part == 1, 2 * late, 2 * early)
            unit(j, 1, pl.ds(pl.multiple_of(part * W, W), W), j + (1 - part) * room)
            return 0

        lax.fori_loop(0, late_left + early_left, single, 0)


    def crawl(self, unit):
        room = NX * len(self.groups)

        def one(k, _):
            half = lax.rem(k, 2)
            k = k // 2
            part = (k < self.late).astype(jnp.int32)
            j = k - (1 - part) * self.late
            unit(j, pl.ds(pl.multiple_of(part * W + half * 512, 512), 512), j + (1 - part) * room, half)
            return 0

        lax.fori_loop(0, 2 * (self.late + self.early), one, 0)


def fold(k, vt, qt, ml, ot, sl, mask=None):
    s = dot(k, qt[:, sl]) * C2
    if mask is not None:
        s = jnp.where(mask, s, NEG)
    old = ml[0:1, sl]
    m = jnp.maximum(old, jnp.max(s, axis=0, keepdims=True))
    p = jnp.exp2(s - m)
    a = jnp.exp2(old - m)
    ml[0:1, sl] = m
    ml[1:2, sl] = ml[1:2, sl] * a + jnp.sum(p, axis=0, keepdims=True)
    ot[:, sl] = ot[:, sl] * a + dot(vt, p.astype(bf))


def first(kv, qt, ml, ot, sl, mask):
    s = jnp.where(mask, dot(kv[:, 0:128], qt[:, sl]) * C2, NEG)
    m = jnp.max(s, axis=0, keepdims=True)
    p = jnp.exp2(s - m)
    ml[0:1, sl] = m
    ml[1:2, sl] = jnp.sum(p, axis=0, keepdims=True)
    ot[:, sl] = dot(flip(kv[:, 128:256]), p.astype(bf))


def fold_groups(sc_ref, groups, qt, ml, ot, ml_old, ot_old, vs, kt, ps, ks, vt):
    ml[...] = ml_old[...]
    ot[...] = ot_old[...]
    plan = Plan(sc_ref, groups)

    def prepare(j, kv):
        ks[chunks(j), :] = kv[:, 0:128]
        vs[chunks(j), :] = kv[:, 128:256]
        kt[:, chunks(j)] = flip(kv[:, 0:128])
        vt[:, chunks(j)] = flip(kv[:, 128:256])

    plan.each(prepare)

    def unit(j, n, sl, at):
        p = jnp.exp2(dot(ks[chunks(j, n), :], qt[:, sl]) * C2 - ml[0:1, sl])
        rounded = p.astype(bf)
        ps[chunks(at, n), :] = rounded
        ml[1:2, sl] = ml[1:2, sl] + jnp.sum(p, axis=0, keepdims=True)
        ot[:, sl] = ot[:, sl] + dot(vt[:, chunks(j, n)], rounded)

    plan.sweep(unit)

    @pl.when(jnp.logical_not(jnp.max(ml[1:2, :]) < 2.0**64))
    def _():
        ml[...] = ml_old[...]
        ot[...] = ot_old[...]

        def slow(j, sl, at, half):
            fold(ks[chunks(j), :], vt[:, chunks(j)], qt, ml, ot, sl)

        def again(j, sl, at, half):
            p = jnp.exp2(dot(ks[chunks(j), :], qt[:, sl]) * C2 - ml[0:1, sl])
            ps[chunks(at), pl.ds(pl.multiple_of(half * 512, 512), 512)] = p.astype(bf)

        plan.crawl(slow)
        plan.crawl(again)

    ml[3:4, :] = ml[0:1, :]


def begin_kernel(sc_ref, qd_ref, kv_ref, nkv_ref, qt, dt, rows, ml_out, ot_out, vs, kt, ps, ks, vt, ml, ot):
    for sl, here, at in tiles():
        q = qd_ref[here, at]
        d = qd_ref[here, 1024 + at.start : 1024 + at.stop]
        rows[sl, 0:128] = q
        rows[sl, 128:256] = d
        qt[:, sl] = flip(q)
        dt[:, sl] = flip(d)
    ml[...] = jnp.zeros_like(ml)
    kb, rb = masks()
    for part in range(2):
        own = kv_ref[sc_ref[part]]
        first(own, qt, ml, ot, cols(part, 0), kb <= rb)
        first(nkv_ref[part], qt, ml, ot, cols(part, 1), kb == rb)
        fold(own[:, 0:128], flip(own[:, 128:256]), qt, ml, ot, cols(part, 1), kb < rb)
    fold_groups(sc_ref, [(0, kv_ref)], qt, ml_out, ot_out, ml, ot, vs, kt, ps, ks, vt)


def more_kernel(offsets, sc_ref, qt, ml_in, ot_in, ka_ref, kb_ref, ml, ot, vs, kt, ps, ks, vt):
    fold_groups(sc_ref, list(zip(offsets, (ka_ref, kb_ref))), qt, ml, ot, ml_in, ot_in, vs, kt, ps, ks, vt)


def last_kernel(sc_ref, qt, dt, ml_in, ot_in, ka_ref, kb_ref, ml, o_ref, vs, kt, ps, kv, ot, ks, vt):
    kv[0:2] = ka_ref[...]
    kv[2:4] = kb_ref[...]
    fold_groups(sc_ref, [(4, kv)], qt, ml, ot, ml_in, ot_in, vs, kt, ps, ks, vt)
    total = ml[1:2, :]
    inverse = 1.0 / total
    ml[0:1, :] = ml[0:1, :] + jnp.log2(total)
    for sl, here, at in tiles():
        o = ot[:, sl] * inverse[:, sl]
        ml[2:3, sl] = jnp.sum(o * dt[:, sl].astype(f32), axis=0, keepdims=True)
        o_ref[here, at] = o.T.astype(bf)


def grads(k, v, kt, qt, dt, rows, ml, dq, sl, mask=None):
    s = dot(k, qt[:, sl]) * C2
    if mask is not None:
        s = jnp.where(mask, s, NEG)
    p = jnp.exp2(s - ml[0:1, sl])
    ds = (p * (dot(v, dt[:, sl]) - ml[2:3, sl])).astype(bf)
    dq[:, sl] = dq[:, sl] + dot(kt, ds)
    return dot(ds, rows[sl, 0:128]), dot(p.astype(bf), rows[sl, 128:256])


def grad_groups(sc_ref, offsets, dt, rows, ml, dq, mk, vs, kt, ps, acc):
    plan = Plan(sc_ref, [(offset, None) for offset in offsets])

    def unit(j, n, sl, at):
        keys = chunks(j, n)
        p = ps[chunks(at, n), :].astype(f32) * jnp.exp2(mk[3:4, sl] - ml[0:1, sl])
        ds = (p * (dot(vs[keys, :], dt[:, sl]) - ml[2:3, sl])).astype(bf)
        dq[:, sl] = dq[:, sl] + dot(kt[:, keys], ds)
        opening = at == j
        acc[keys, 0:128] = jnp.where(opening, 0.0, acc[keys, 0:128]) + dot(ds, rows[sl, 0:128])
        acc[keys, 128:256] = jnp.where(opening, 0.0, acc[keys, 128:256]) + dot(p.astype(bf), rows[sl, 128:256])

    plan.sweep(unit)
    return plan


def hand_over(plan, acc, outs):
    for g, put in enumerate(outs):
        high = plan.bounds[g][1]

        def some(i, _):
            j = chunks(plan.place(g, i))
            put(i, jnp.concatenate([acc[j, 0:128] * SC, acc[j, 128:256]], axis=1).astype(bf))
            return 0

        def none(i, _):
            put(i, jnp.zeros((C, 256), bf))
            return 0

        lax.fori_loop(0, high, some, 0)
        lax.fori_loop(high, NX, none, 0)


def into(ref):
    def put(i, value):
        ref[i] = value

    return put


def far_kernel(sc_ref, dt, rows, ml, mk, vs, kt, ps, dq, oa, ob, acc, out):
    dq[...] = jnp.zeros_like(dq)
    plan = grad_groups(sc_ref, (4,), dt, rows, ml, dq, mk, vs, kt, ps, acc)
    hand_over(plan, acc, [into(out)])
    oa[...] = out[0:2]
    ob[...] = out[2:4]


def pair_kernel(offsets, sc_ref, dt, rows, ml, dq_in, mk, vs, kt, ps, dq, oa, ob, acc):
    dq[...] = dq_in[...]
    plan = grad_groups(sc_ref, offsets, dt, rows, ml, dq, mk, vs, kt, ps, acc)
    hand_over(plan, acc, [into(oa), into(ob)])


def own_kernel(sc_ref, dt, rows, ml, dq_in, mk, vs, kt, ps, qt, kv_ref, nkv_ref, keep_ref, dq, out, acc):
    dq[...] = dq_in[...]
    plan = grad_groups(sc_ref, (0,), dt, rows, ml, dq, mk, vs, kt, ps, acc)
    kb, rb = masks()
    seen_own = jnp.concatenate([(rb - kb).astype(f32), (rb - kb - 1).astype(f32)], axis=1) >= 0
    for part in range(2):
        i = sc_ref[part]
        own, noised = kv_ref[i], nkv_ref[part]
        k, v, turned = own[:, 0:128], own[:, 128:256], flip(own[:, 0:128])
        ko, vo = grads(k, v, turned, qt, dt, rows, ml, dq, slice(part * W, part * W + W), seen_own)
        k, v, turned = noised[:, 0:128], noised[:, 128:256], flip(noised[:, 0:128])
        kn, vn = grads(k, v, turned, qt, dt, rows, ml, dq, cols(part, 1), kb == rb)
        keep = keep_ref[part]
        seen = i < plan.late
        before = acc[chunks(i), :]
        acc[chunks(i), 0:128] = jnp.where(seen, before[:, 0:128], 0.0) + ko + kn * keep
        acc[chunks(i), 128:256] = jnp.where(seen, before[:, 128:256], 0.0) + vo + vn * keep
    plan.bounds = [(plan.bounds[0][0], plan.bounds[0][1] + 1)]

    hand_over(plan, acc, [into(out)])


def near_grads_kernel(sc_ref, dt, rows, ml, dq_in, mk, vs, kt, ps, o_rows, q_rows, oa, ob, dq, acc):
    pair_kernel((7, 1), sc_ref, dt, rows, ml, dq_in, mk, vs, kt, ps, dq, oa, ob, acc)
    q_rows[:, 0:1024] = o_rows[...]
    for sl, here, at in tiles():
        q_rows[here, 1024 + at.start : 1024 + at.stop] = (dq[:, sl] * SC).T.astype(bf)


def unpack_kv_kernel(sc_ref, got, dk, dv):
    for h in range(NH):
        total = got[h].astype(f32)
        for x in range(1, NX):
            total = total + got[x * NH + h].astype(f32)
        dk[:, h * 128 : h * 128 + 128] = total[:, 0:128].astype(bf)
        dv[:, h * 128 : h * 128 + 128] = total[:, 128:256].astype(bf)


def call(body, name, outs, args, scratch):
    vm = pl.BlockSpec(memory_space=pltpu.VMEM)
    return pl.pallas_call(
        body,
        out_shape=tuple(jax.ShapeDtypeStruct(*o) for o in outs),
        in_specs=[pl.BlockSpec(memory_space=pltpu.SMEM)] + [vm] * (len(args) - 1),
        out_specs=(vm,) * len(outs),
        scratch_shapes=[pltpu.VMEM(*s) for s in scratch],
        compiler_params=pltpu.CompilerParams(vmem_limit_bytes=20 * 1024 * 1024),
        cost_estimate=pl.CostEstimate(flops=200_000_000, bytes_accessed=1_000_000, transcendentals=1_000_000),
        name=name,
    )(*args)


def device(x, z, h):
    return (x * NZ + z) * NH + h


BOTH = ("ctx", "head")
PLANE = [[device(x, z, h) for x in range(NX) for h in range(NH)] for z in range(NZ)]
MIRROR = [[device(x, z, h) for x in (a, NX - 1 - a) for h in range(NH)] for z in range(NZ) for a in range(2)]
UP = [(x * NZ + z, x * NZ + (z + 1) % NZ) for x in range(NX) for z in range(NZ)]
DOWN = [(x * NZ + z, x * NZ + (z - 1) % NZ) for x in range(NX) for z in range(NZ)]
SWAP = [(x * NZ + z, (NX - 1 - x) * NZ + z) for x in range(NX) for z in range(NZ)]


def exchange(a, groups):
    return lax.all_to_all(a, BOTH, split_axis=0, concat_axis=0, tiled=True, axis_index_groups=groups)


def up(a):
    return lax.ppermute(a, "ctx", UP)


def down(a):
    return lax.ppermute(a, "ctx", DOWN)


def spread(parts):
    cut = [jnp.transpose(p.reshape(2, 16, NH, 512), (0, 2, 1, 3)) for p in parts]
    sent = jnp.concatenate(cut, axis=3).reshape(16, 16, -1)
    return exchange(sent, MIRROR).reshape(256, -1)


def collect(rows, parts):
    got = exchange(rows.reshape(16, 16, -1), MIRROR).reshape(2, NH, 16, parts, 512)
    return tuple(jnp.transpose(got[:, :, :, i], (0, 2, 1, 3)).reshape(32, -1) for i in range(parts))


def on_device(q_clean, k_clean, v_clean, q_noised, masked, noise_level, mask_key, mask_value, d_clean, d_noised):
    ctx = lax.axis_index("ctx")
    x, z = ctx // NZ, ctx % NZ
    lo = jnp.minimum(x, NX - 1 - x)
    sc = jnp.stack([lo, NX - 1 - lo, z]).astype(jnp.int32)

    kv = jnp.concatenate([k_clean, v_clean], axis=1).reshape(32, 2, NH, 128)
    kv = jnp.broadcast_to(jnp.transpose(kv, (2, 0, 1, 3)).reshape(NH, 32, 256)[None], (NX, NH, 32, 256)).reshape(NX * NH, 32, 256)
    here = exchange(kv, PLANE).reshape(NX, C, 256)
    qd = spread((q_clean, q_noised, d_clean, d_noised))
    info = jnp.concatenate([masked, noise_level])
    other = lax.ppermute(info, "ctx", SWAP)
    info = jnp.where(x < 2, jnp.stack([info, other]), jnp.stack([other, info]))
    covered = info[:, :C] == 1
    onehot = (info[:, C:, None] == jnp.arange(LEVELS, dtype=jnp.int32)).astype(bf)
    table = dot(onehot.reshape(16, LEVELS), jnp.concatenate([mask_key, mask_value], axis=1)).astype(bf)
    table = jnp.repeat(table, BLOCK, axis=0).reshape(2, C, 256)
    mine = jnp.stack([lax.dynamic_index_in_dim(here, sc[i], 0, keepdims=False) for i in range(2)])
    nkv = jnp.where(covered[:, :, None], table, mine)
    keep = jnp.broadcast_to((info[:, :C] == 0).astype(f32)[:, :, None], (2, C, 128))

    a1, b1 = up(here), down(here)
    a2, b2 = up(a1), down(b1)
    state = [((8, 2 * W), f32), ((128, 2 * W), f32)]
    turned = ((128, 2 * W), bf)
    part = ((NX, C, 256), bf)
    half = ((2, C, 256), bf)
    keys = [((8 * C, 128), bf), ((128, 8 * C), bf)]
    one, two = keys + [((6 * C, W), bf)], keys + [((12 * C, W), bf)]
    acc = [((8 * C, 256), f32)]
    qt, dt, rows, ml0, ot, *keys0 = call(
        begin_kernel, "begin", [turned, turned, ((2 * W, 256), bf)] + state + one, (sc, qd, here, nkv), keys + state
    )
    a2, b2, ml0 = lax.optimization_barrier((a2, b2, ml0))
    a3, b3 = up(a2), down(b2)
    ml1, ot, *keys1 = call(functools.partial(more_kernel, (7, 1)), "near", state + two, (sc, qt, ml0, ot, a1, b1), keys)
    ml2, ot, *keys2 = call(functools.partial(more_kernel, (6, 2)), "second", state + two, (sc, qt, ml1, ot, a2, b2), keys)
    a3, b3, ml2 = lax.optimization_barrier((a3, b3, ml2))
    a4, b4 = up(a3[0:2]), down(b3[2:4])
    ml3, ot, *keys3 = call(functools.partial(more_kernel, (5, 3)), "third", state + two, (sc, qt, ml2, ot, a3, b3), keys)
    ml, o_rows, *keys4 = call(
        last_kernel, "finish", [state[0], ((256, 1024), bf)] + one, (sc, qt, dt, ml3, ot, a4, b4), [part, state[1]] + keys
    )
    fixed = (sc, dt, rows, ml)
    dq_state = state[1]
    dq, ga, gb = call(far_kernel, "back4", [dq_state, half, half], fixed + (ml, *keys4), acc + [part])
    ga, gb = up(ga), down(gb)
    back = [dq_state, part, part]
    dq, pb, pa = call(functools.partial(pair_kernel, (5, 3)), "back3", back, fixed + (dq, ml3, *keys3), acc)
    ga = jnp.concatenate([pa[0:2] + ga, pa[2:4]], axis=0)
    gb = jnp.concatenate([pb[0:2], pb[2:4] + gb], axis=0)
    dq, ga, gb = lax.optimization_barrier((dq, ga, gb))
    ga, gb = up(ga), down(gb)
    dq, pb, pa = call(functools.partial(pair_kernel, (6, 2)), "back2", back, fixed + (dq, ml2, *keys2), acc)
    dq, ga, gb = lax.optimization_barrier((dq, pa + ga, pb + gb))
    ga, gb = up(ga), down(gb)
    dq, own = call(own_kernel, "back0", [dq_state, part], fixed + (dq, ml0, *keys0, qt, here, nkv, keep), acc)
    q_rows, pb, pa = call(
        near_grads_kernel, "back1", [((256, 2048), bf), part, part], fixed + (dq, ml1, *keys1, o_rows), [dq_state] + acc
    )
    q_rows, ga, gb = lax.optimization_barrier((q_rows, pa + ga, pb + gb))
    ga, gb = up(ga), down(gb)
    outs = collect(q_rows, 4)
    total = (own.astype(f32) + ga.astype(f32) + gb.astype(f32)).astype(bf)
    got = exchange(total.reshape(NX * NH, 32, 256), PLANE)
    return outs + tuple(call(unpack_kv_kernel, "unpack_kv", [((32, 1024), bf)] * 2, (sc, got), []))


def solution(mesh):
    tokens = P(("ctx", "head"), None)
    return jax.shard_map(
        on_device,
        mesh=mesh,
        in_specs=(tokens,) * 4 + (P("ctx"), P("ctx"), P(None, "head"), P(None, "head"), tokens, tokens),
        out_specs=(tokens,) * 6,
        check_vma=False,
    )
```

```python
import functools
import math

import jax
import jax.numpy as jnp
from jax import lax
from jax.experimental import pallas as pl
from jax.experimental.pallas import tpu as pltpu
from jax.sharding import PartitionSpec as P

bf = jnp.bfloat16
f32 = jnp.float32
BLOCK = 32
LEVELS = 8
NX, NZ, NH = 4, 8, 8
C = 256
W = 1024
NEG = -1e30
SC = 1.0 / math.sqrt(128)
C2 = math.log2(math.e) * SC


def dot(a, b):
    return jnp.dot(a, b, preferred_element_type=f32)


def flip(a):
    return a.T


def cols(part, stream):
    return slice(part * W + stream * 512, part * W + stream * 512 + 512)


def tiles():
    for part in range(2):
        for t in range(8):
            at = part * W + t * 128
            yield slice(at, at + 128), slice(part * 128, part * 128 + 128), slice(t * 128, t * 128 + 128)


def masks():
    key_block = lax.broadcasted_iota(jnp.int32, (C, 512), 0) // BLOCK
    row_block = (lax.broadcasted_iota(jnp.int32, (C, 512), 1) % 128) // 16
    return key_block, row_block


def chunks(j, n=1):
    return pl.ds(pl.multiple_of(j * C, C), n * C)


def group_bounds(sc_ref, offset):
    z = sc_ref[2]
    earlier = (lax.rem(z + offset, NZ) < z).astype(jnp.int32)
    return sc_ref[0] + earlier, sc_ref[1] + earlier


class Plan:
    def __init__(self, sc_ref, groups):
        self.groups = [kv_ref for _, kv_ref in groups]
        self.bounds = [group_bounds(sc_ref, offset) for offset, _ in groups]
        self.early = sum(low for low, _ in self.bounds)
        self.late = sum(high for _, high in self.bounds)

    def place(self, g, i):
        low, _ = self.bounds[g]
        low_base, high_base = 0, self.early
        if g:
            low_base = self.bounds[0][0]
            high_base = self.early + self.bounds[0][1] - self.bounds[0][0]
        return jnp.where(i < low, low_base + i, high_base + i - low)

    def each(self, body):
        for g, kv_ref in enumerate(self.groups):

            def one(i, _):
                body(self.place(g, i), kv_ref[i])
                return 0

            lax.fori_loop(0, self.bounds[g][1], one, 0)

    def sweep(self, unit):
        room = NX * len(self.groups)
        late, early = self.late // 2, self.early // 2

        def double(k, _):
            part = (k < late).astype(jnp.int32)
            j = jnp.where(part == 1, k, k - late) * 2
            unit(j, 2, pl.ds(pl.multiple_of(part * W, W), W), j + (1 - part) * room)
            return 0

        lax.fori_loop(0, late + early, double, 0)
        late_left, early_left = self.late - 2 * late, self.early - 2 * early

        def single(k, _):
            part = (k < late_left).astype(jnp.int32)
            j = jnp.where(part == 1, 2 * late, 2 * early)
            unit(j, 1, pl.ds(pl.multiple_of(part * W, W), W), j + (1 - part) * room)
            return 0

        lax.fori_loop(0, late_left + early_left, single, 0)


    def crawl(self, unit):
        room = NX * len(self.groups)

        def one(k, _):
            half = lax.rem(k, 2)
            k = k // 2
            part = (k < self.late).astype(jnp.int32)
            j = k - (1 - part) * self.late
            unit(j, pl.ds(pl.multiple_of(part * W + half * 512, 512), 512), j + (1 - part) * room, half)
            return 0

        lax.fori_loop(0, 2 * (self.late + self.early), one, 0)


def fold(k, vt, qt, ml, ot, sl, mask=None):
    s = dot(k, qt[:, sl]) * C2
    if mask is not None:
        s = jnp.where(mask, s, NEG)
    old = ml[0:1, sl]
    m = jnp.maximum(old, jnp.max(s, axis=0, keepdims=True))
    p = jnp.exp2(s - m)
    a = jnp.exp2(old - m)
    ml[0:1, sl] = m
    ml[1:2, sl] = ml[1:2, sl] * a + jnp.sum(p, axis=0, keepdims=True)
    ot[:, sl] = ot[:, sl] * a + dot(vt, p.astype(bf))


def first(kv, qt, ml, ot, sl, mask):
    s = jnp.where(mask, dot(kv[:, 0:128], qt[:, sl]) * C2, NEG)
    m = jnp.max(s, axis=0, keepdims=True)
    p = jnp.exp2(s - m)
    ml[0:1, sl] = m
    ml[1:2, sl] = jnp.sum(p, axis=0, keepdims=True)
    ot[:, sl] = dot(flip(kv[:, 128:256]), p.astype(bf))


def fold_groups(sc_ref, groups, qt, ml, ot, ml_old, ot_old, vs, kt, ps, ks, vt):
    ml[...] = ml_old[...]
    ot[...] = ot_old[...]
    plan = Plan(sc_ref, groups)

    def prepare(j, kv):
        ks[chunks(j), :] = kv[:, 0:128]
        vs[chunks(j), :] = kv[:, 128:256]
        kt[:, chunks(j)] = flip(kv[:, 0:128])
        vt[:, chunks(j)] = flip(kv[:, 128:256])

    plan.each(prepare)

    def unit(j, n, sl, at):
        p = jnp.exp2(dot(ks[chunks(j, n), :], qt[:, sl]) * C2 - ml[0:1, sl])
        rounded = p.astype(bf)
        ps[chunks(at, n), :] = rounded
        ml[1:2, sl] = ml[1:2, sl] + jnp.sum(p, axis=0, keepdims=True)
        ot[:, sl] = ot[:, sl] + dot(vt[:, chunks(j, n)], rounded)

    plan.sweep(unit)

    @pl.when(jnp.logical_not(jnp.max(ml[1:2, :]) < 2.0**64))
    def _():
        ml[...] = ml_old[...]
        ot[...] = ot_old[...]

        def slow(j, sl, at, half):
            fold(ks[chunks(j), :], vt[:, chunks(j)], qt, ml, ot, sl)

        def again(j, sl, at, half):
            p = jnp.exp2(dot(ks[chunks(j), :], qt[:, sl]) * C2 - ml[0:1, sl])
            ps[chunks(at), pl.ds(pl.multiple_of(half * 512, 512), 512)] = p.astype(bf)

        plan.crawl(slow)
        plan.crawl(again)

    ml[3:4, :] = ml[0:1, :]


def begin_kernel(sc_ref, qd_ref, kv_ref, nkv_ref, qt, dt, rows, ml_out, ot_out, vs, kt, ps, ks, vt, ml, ot):
    for sl, here, at in tiles():
        q = qd_ref[here, at]
        d = qd_ref[here, 1024 + at.start : 1024 + at.stop]
        rows[sl, 0:128] = q
        rows[sl, 128:256] = d
        qt[:, sl] = flip(q)
        dt[:, sl] = flip(d)
    ml[...] = jnp.zeros_like(ml)
    kb, rb = masks()
    for part in range(2):
        own = kv_ref[sc_ref[part]]
        first(own, qt, ml, ot, cols(part, 0), kb <= rb)
        first(nkv_ref[part], qt, ml, ot, cols(part, 1), kb == rb)
        fold(own[:, 0:128], flip(own[:, 128:256]), qt, ml, ot, cols(part, 1), kb < rb)
    fold_groups(sc_ref, [(0, kv_ref)], qt, ml_out, ot_out, ml, ot, vs, kt, ps, ks, vt)


def more_kernel(offsets, sc_ref, qt, ml_in, ot_in, ka_ref, kb_ref, ml, ot, vs, kt, ps, ks, vt):
    fold_groups(sc_ref, list(zip(offsets, (ka_ref, kb_ref))), qt, ml, ot, ml_in, ot_in, vs, kt, ps, ks, vt)


def last_kernel(sc_ref, qt, dt, ml_in, ot_in, ka_ref, kb_ref, ml, o_ref, vs, kt, ps, kv, ot, ks, vt):
    kv[0:2] = ka_ref[...]
    kv[2:4] = kb_ref[...]
    fold_groups(sc_ref, [(4, kv)], qt, ml, ot, ml_in, ot_in, vs, kt, ps, ks, vt)
    total = ml[1:2, :]
    inverse = 1.0 / total
    ml[0:1, :] = ml[0:1, :] + jnp.log2(total)
    for sl, here, at in tiles():
        o = ot[:, sl] * inverse[:, sl]
        ml[2:3, sl] = jnp.sum(o * dt[:, sl].astype(f32), axis=0, keepdims=True)
        o_ref[here, at] = o.astype(bf).T


def grads(k, v, kt, qt, dt, rows, ml, dq, sl, mask=None):
    s = dot(k, qt[:, sl]) * C2
    if mask is not None:
        s = jnp.where(mask, s, NEG)
    p = jnp.exp2(s - ml[0:1, sl])
    ds = (p * (dot(v, dt[:, sl]) - ml[2:3, sl])).astype(bf)
    dq[:, sl] = dq[:, sl] + dot(kt, ds)
    return dot(ds, rows[sl, 0:128]), dot(p.astype(bf), rows[sl, 128:256])


def grad_groups(sc_ref, offsets, dt, rows, ml, dq, mk, vs, kt, ps, acc):
    plan = Plan(sc_ref, [(offset, None) for offset in offsets])

    def unit(j, n, sl, at):
        keys = chunks(j, n)
        p = ps[chunks(at, n), :].astype(f32) * jnp.exp2(mk[3:4, sl] - ml[0:1, sl])
        ds = (p * (dot(vs[keys, :], dt[:, sl]) - ml[2:3, sl])).astype(bf)
        dq[:, sl] = dq[:, sl] + dot(kt[:, keys], ds)
        opening = at == j
        acc[keys, 0:128] = jnp.where(opening, 0.0, acc[keys, 0:128]) + dot(ds, rows[sl, 0:128])
        acc[keys, 128:256] = jnp.where(opening, 0.0, acc[keys, 128:256]) + dot(p.astype(bf), rows[sl, 128:256])

    plan.sweep(unit)
    return plan


def hand_over(plan, acc, outs):
    for g, put in enumerate(outs):
        high = plan.bounds[g][1]

        def some(i, _):
            j = chunks(plan.place(g, i))
            put(i, jnp.concatenate([acc[j, 0:128] * SC, acc[j, 128:256]], axis=1).astype(bf))
            return 0

        def none(i, _):
            put(i, jnp.zeros((C, 256), bf))
            return 0

        lax.fori_loop(0, high, some, 0)
        lax.fori_loop(high, NX, none, 0)


def into(ref):
    def put(i, value):
        ref[i] = value

    return put


def far_kernel(sc_ref, dt, rows, ml, mk, vs, kt, ps, dq, oa, ob, acc, out):
    dq[...] = jnp.zeros_like(dq)
    plan = grad_groups(sc_ref, (4,), dt, rows, ml, dq, mk, vs, kt, ps, acc)
    hand_over(plan, acc, [into(out)])
    oa[...] = out[0:2]
    ob[...] = out[2:4]


def pair_kernel(offsets, sc_ref, dt, rows, ml, dq_in, mk, vs, kt, ps, dq, oa, ob, acc):
    dq[...] = dq_in[...]
    plan = grad_groups(sc_ref, offsets, dt, rows, ml, dq, mk, vs, kt, ps, acc)
    hand_over(plan, acc, [into(oa), into(ob)])


def own_kernel(sc_ref, dt, rows, ml, dq_in, mk, vs, kt, ps, qt, kv_ref, nkv_ref, keep_ref, dq, out, acc):
    dq[...] = dq_in[...]
    plan = grad_groups(sc_ref, (0,), dt, rows, ml, dq, mk, vs, kt, ps, acc)
    kb, rb = masks()
    seen_own = jnp.concatenate([(rb - kb).astype(f32), (rb - kb - 1).astype(f32)], axis=1) >= 0
    for part in range(2):
        i = sc_ref[part]
        own, noised = kv_ref[i], nkv_ref[part]
        k, v, turned = own[:, 0:128], own[:, 128:256], flip(own[:, 0:128])
        ko, vo = grads(k, v, turned, qt, dt, rows, ml, dq, slice(part * W, part * W + W), seen_own)
        k, v, turned = noised[:, 0:128], noised[:, 128:256], flip(noised[:, 0:128])
        kn, vn = grads(k, v, turned, qt, dt, rows, ml, dq, cols(part, 1), kb == rb)
        keep = keep_ref[part]
        seen = i < plan.late
        before = acc[chunks(i), :]
        acc[chunks(i), 0:128] = jnp.where(seen, before[:, 0:128], 0.0) + ko + kn * keep
        acc[chunks(i), 128:256] = jnp.where(seen, before[:, 128:256], 0.0) + vo + vn * keep
    plan.bounds = [(plan.bounds[0][0], plan.bounds[0][1] + 1)]

    hand_over(plan, acc, [into(out)])


def near_grads_kernel(sc_ref, dt, rows, ml, dq_in, mk, vs, kt, ps, o_rows, q_rows, oa, ob, dq, acc):
    pair_kernel((7, 1), sc_ref, dt, rows, ml, dq_in, mk, vs, kt, ps, dq, oa, ob, acc)
    q_rows[:, 0:1024] = o_rows[...]
    for sl, here, at in tiles():
        q_rows[here, 1024 + at.start : 1024 + at.stop] = (dq[:, sl] * SC).astype(bf).T


def unpack_kv_kernel(sc_ref, got, dk, dv):
    for h in range(NH):
        total = got[h].astype(f32)
        for x in range(1, NX):
            total = total + got[x * NH + h].astype(f32)
        dk[:, h * 128 : h * 128 + 128] = total[:, 0:128].astype(bf)
        dv[:, h * 128 : h * 128 + 128] = total[:, 128:256].astype(bf)


def call(body, name, outs, args, scratch):
    vm = pl.BlockSpec(memory_space=pltpu.VMEM)
    return pl.pallas_call(
        body,
        out_shape=tuple(jax.ShapeDtypeStruct(*o) for o in outs),
        in_specs=[pl.BlockSpec(memory_space=pltpu.SMEM)] + [vm] * (len(args) - 1),
        out_specs=(vm,) * len(outs),
        scratch_shapes=[pltpu.VMEM(*s) for s in scratch],
        compiler_params=pltpu.CompilerParams(vmem_limit_bytes=20 * 1024 * 1024),
        cost_estimate=pl.CostEstimate(flops=200_000_000, bytes_accessed=1_000_000, transcendentals=1_000_000),
        name=name,
    )(*args)


def device(x, z, h):
    return (x * NZ + z) * NH + h


BOTH = ("ctx", "head")
PLANE = [[device(x, z, h) for x in range(NX) for h in range(NH)] for z in range(NZ)]
MIRROR = [[device(x, z, h) for x in (a, NX - 1 - a) for h in range(NH)] for z in range(NZ) for a in range(2)]
UP = [(x * NZ + z, x * NZ + (z + 1) % NZ) for x in range(NX) for z in range(NZ)]
DOWN = [(x * NZ + z, x * NZ + (z - 1) % NZ) for x in range(NX) for z in range(NZ)]
SWAP = [(x * NZ + z, (NX - 1 - x) * NZ + z) for x in range(NX) for z in range(NZ)]


def exchange(a, groups):
    return lax.all_to_all(a, BOTH, split_axis=0, concat_axis=0, tiled=True, axis_index_groups=groups)


def up(a):
    return lax.ppermute(a, "ctx", UP)


def down(a):
    return lax.ppermute(a, "ctx", DOWN)


def spread(parts):
    cut = [jnp.transpose(p.reshape(2, 16, NH, 512), (0, 2, 1, 3)) for p in parts]
    sent = jnp.concatenate(cut, axis=3).reshape(16, 16, -1)
    return exchange(sent, MIRROR).reshape(256, -1)


def collect(rows, parts):
    got = exchange(rows.reshape(16, 16, -1), MIRROR).reshape(2, NH, 16, parts, 512)
    return tuple(jnp.transpose(got[:, :, :, i], (0, 2, 1, 3)).reshape(32, -1) for i in range(parts))


def on_device(q_clean, k_clean, v_clean, q_noised, masked, noise_level, mask_key, mask_value, d_clean, d_noised):
    ctx = lax.axis_index("ctx")
    x, z = ctx // NZ, ctx % NZ
    lo = jnp.minimum(x, NX - 1 - x)
    sc = jnp.stack([lo, NX - 1 - lo, z]).astype(jnp.int32)

    kv = jnp.concatenate([k_clean, v_clean], axis=1).reshape(32, 2, NH, 128)
    kv = jnp.broadcast_to(jnp.transpose(kv, (2, 0, 1, 3)).reshape(NH, 32, 256)[None], (NX, NH, 32, 256)).reshape(NX * NH, 32, 256)
    here = exchange(kv, PLANE).reshape(NX, C, 256)
    qd = spread((q_clean, q_noised, d_clean, d_noised))
    info = jnp.concatenate([masked, noise_level])
    other = lax.ppermute(info, "ctx", SWAP)
    info = jnp.where(x < 2, jnp.stack([info, other]), jnp.stack([other, info]))
    covered = info[:, :C] == 1
    onehot = (info[:, C:, None] == jnp.arange(LEVELS, dtype=jnp.int32)).astype(bf)
    table = dot(onehot.reshape(16, LEVELS), jnp.concatenate([mask_key, mask_value], axis=1)).astype(bf)
    table = jnp.repeat(table, BLOCK, axis=0).reshape(2, C, 256)
    mine = jnp.stack([lax.dynamic_index_in_dim(here, sc[i], 0, keepdims=False) for i in range(2)])
    nkv = jnp.where(covered[:, :, None], table, mine)
    keep = jnp.broadcast_to((info[:, :C] == 0).astype(f32)[:, :, None], (2, C, 128))

    a1, b1 = up(here), down(here)
    a2, b2 = up(a1), down(b1)
    state = [((8, 2 * W), f32), ((128, 2 * W), f32)]
    turned = ((128, 2 * W), bf)
    part = ((NX, C, 256), bf)
    half = ((2, C, 256), bf)
    keys = [((8 * C, 128), bf), ((128, 8 * C), bf)]
    one, two = keys + [((6 * C, W), bf)], keys + [((12 * C, W), bf)]
    acc = [((8 * C, 256), f32)]
    qt, dt, rows, ml0, ot, *keys0 = call(
        begin_kernel, "begin", [turned, turned, ((2 * W, 256), bf)] + state + one, (sc, qd, here, nkv), keys + state
    )
    a2, b2, ml0 = lax.optimization_barrier((a2, b2, ml0))
    a3, b3 = up(a2), down(b2)
    ml1, ot, *keys1 = call(functools.partial(more_kernel, (7, 1)), "near", state + two, (sc, qt, ml0, ot, a1, b1), keys)
    ml2, ot, *keys2 = call(functools.partial(more_kernel, (6, 2)), "second", state + two, (sc, qt, ml1, ot, a2, b2), keys)
    a3, b3, ml2 = lax.optimization_barrier((a3, b3, ml2))
    a4, b4 = up(a3[0:2]), down(b3[2:4])
    ml3, ot, *keys3 = call(functools.partial(more_kernel, (5, 3)), "third", state + two, (sc, qt, ml2, ot, a3, b3), keys)
    ml, o_rows, *keys4 = call(
        last_kernel, "finish", [state[0], ((256, 1024), bf)] + one, (sc, qt, dt, ml3, ot, a4, b4), [part, state[1]] + keys
    )
    fixed = (sc, dt, rows, ml)
    dq_state = state[1]
    dq, ga, gb = call(far_kernel, "back4", [dq_state, half, half], fixed + (ml, *keys4), acc + [part])
    ga, gb = up(ga), down(gb)
    back = [dq_state, part, part]
    dq, pb, pa = call(functools.partial(pair_kernel, (5, 3)), "back3", back, fixed + (dq, ml3, *keys3), acc)
    ga = jnp.concatenate([pa[0:2] + ga, pa[2:4]], axis=0)
    gb = jnp.concatenate([pb[0:2], pb[2:4] + gb], axis=0)
    dq, ga, gb = lax.optimization_barrier((dq, ga, gb))
    ga, gb = up(ga), down(gb)
    dq, pb, pa = call(functools.partial(pair_kernel, (6, 2)), "back2", back, fixed + (dq, ml2, *keys2), acc)
    dq, ga, gb = lax.optimization_barrier((dq, pa + ga, pb + gb))
    ga, gb = up(ga), down(gb)
    dq, own = call(own_kernel, "back0", [dq_state, part], fixed + (dq, ml0, *keys0, qt, here, nkv, keep), acc)
    q_rows, pb, pa = call(
        near_grads_kernel, "back1", [((256, 2048), bf), part, part], fixed + (dq, ml1, *keys1, o_rows), [dq_state] + acc
    )
    q_rows, ga, gb = lax.optimization_barrier((q_rows, pa + ga, pb + gb))
    ga, gb = up(ga), down(gb)
    outs = collect(q_rows, 4)
    total = (own.astype(f32) + ga.astype(f32) + gb.astype(f32)).astype(bf)
    got = exchange(total.reshape(NX * NH, 32, 256), PLANE)
    return outs + tuple(call(unpack_kv_kernel, "unpack_kv", [((32, 1024), bf)] * 2, (sc, got), []))


def solution(mesh):
    tokens = P(("ctx", "head"), None)
    return jax.shard_map(
        on_device,
        mesh=mesh,
        in_specs=(tokens,) * 4 + (P("ctx"), P("ctx"), P(None, "head"), P(None, "head"), tokens, tokens),
        out_specs=(tokens,) * 6,
        check_vma=False,
    )
```
